32 devices in a mesh: groups: 2 (over x), wide: 16 (over z, y, core).
Axes of the slice: x: 2, y: 2, z: 4, core: 2. Of those that a mesh axis runs over, the one named last changes fastest.
Arguments:
- frames_in: bfloat16 [128, 256, 768], P(('groups', 'wide')), parts along dimension 0, may hold values from -5 to 5
- qkv_spatial: bfloat16 [768, 2304], replicated, may hold values from -6.5 to 6.5
- out_spatial: bfloat16 [768, 768], replicated, may hold values from -0.21875 to 0.21875
- qkv_temporal: bfloat16 [768, 2304], replicated, may hold values from -6.5 to 6.5
- out_temporal: bfloat16 [768, 768], replicated, may hold values from -0.21875 to 0.21875
Outputs:
- frames_out: bfloat16 [128, 256, 768], P(('groups', 'wide')), parts along dimension 0
The draws below stay inside these ranges and needn't reach their ends.
There are 2 independent parts, one for each index of `groups`. The reference program is written for one: setup_inputs(seed, part) draws one part's arguments, and reference() takes and returns one part's arrays. A program takes and returns all parts, laid end to end along the dimension named above; an argument that names none is the same for every part. Nothing has to cross between parts.
All inputs are finite; a program needn't handle non-finite values.
Results may differ from the reference program's by a relative error of at most 0.008.
Values may be sent and summed in bfloat16 or wider, within the bound.
No kernel may reach another device: no remote copies, remote signals or barrier semaphores. Data moves between devices by JAX's collectives and lax.ppermute only.
A program may use at most 128 MiB of HBM per device.

```python
import jax
import jax.numpy as jnp
from jax import lax

D = 768
HEADS = 12
HEAD_DIM = 64
PATCHES = 256
FRAMES = 64


def draw_frames_in(key, part):
    key_base = jax.random.fold_in(key, 11)
    return jnp.clip(jax.random.normal(key_base, (FRAMES, PATCHES, D), jnp.float32), -5.0, 5.0).astype(jnp.bfloat16)


def projection_draw(key):
    inverse = D ** (-0.5)
    key_query = jax.random.fold_in(key, 21)
    key_key = jax.random.fold_in(key, 22)
    key_value = jax.random.fold_in(key, 23)
    queries = jnp.clip(jax.random.normal(key_query, (D, D), jnp.float32), -4.0, 4.0) * inverse
    values = jnp.clip(jax.random.normal(key_value, (D, D), jnp.float32), -4.0, 4.0) * inverse
    other = jnp.clip(jax.random.normal(key_key, (D, D), jnp.float32), -4.0, 4.0) * inverse
    keys_part = other
    return jnp.concatenate([queries, keys_part, values], axis=1)


def draw_qkv_spatial(key, part):
    return projection_draw(jax.random.fold_in(key, 31)).astype(jnp.bfloat16)


def draw_qkv_temporal(key, part):
    return projection_draw(jax.random.fold_in(key, 32)).astype(jnp.bfloat16)


def bell_draw(own_key, dims, width, bound, held_as=jnp.bfloat16):
    entries = width * jax.random.normal(own_key, dims, jnp.float32)
    return jnp.clip(entries, min=-bound, max=bound).astype(held_as)


def setup_inputs(seed: int = 0, part: int = 0) -> dict:
    keys = jax.random.split(jax.random.key(seed), 6)
    part_splits = jax.random.split(jax.random.fold_in(keys[5], part), 6)
    frames_in = draw_frames_in(jax.random.fold_in(jax.random.fold_in(keys[5], part), 71), part)
    qkv_spatial = draw_qkv_spatial(jax.random.fold_in(keys[5], 71), part)
    out_spatial = bell_draw(keys[2], (D, D), D ** -0.5, 0.21875)
    qkv_temporal = draw_qkv_temporal(jax.random.fold_in(keys[5], 71), part)
    out_temporal = bell_draw(keys[4], (D, D), D ** -0.5, 0.21875)
    return {"frames_in": frames_in, "qkv_spatial": qkv_spatial, "out_spatial": out_spatial, "qkv_temporal": qkv_temporal, "out_temporal": out_temporal}


def normalize(tensor):
    floats = tensor.astype(jnp.float32)
    average = lax.optimization_barrier(jnp.mean(floats, axis=-1, keepdims=True))
    centred = floats - average
    spread = lax.optimization_barrier(jnp.mean(centred * centred, axis=-1, keepdims=True))
    return (centred * lax.rsqrt(spread + 1e-06)).astype(jnp.bfloat16)

def attend_sequence(projected):
    length = projected.shape[0]
    split = projected.astype(jnp.float32).reshape(length, 3, HEADS, HEAD_DIM)
    scores = jnp.einsum('qhd,khd->hqk', split[:, 0], split[:, 1]) * HEAD_DIM ** (-0.5)
    weights = jax.nn.softmax(scores, axis=-1).astype(jnp.bfloat16)
    weights = lax.optimization_barrier(weights).astype(jnp.float32)
    mixed = jnp.einsum('hqk,khd->qhd', weights, split[:, 2])
    return mixed.reshape(length, HEADS * HEAD_DIM).astype(jnp.bfloat16)

def reference(frames_in, qkv_spatial, out_spatial, qkv_temporal, out_temporal):
    first = normalize(frames_in)
    proj_one = jnp.dot(first.reshape(-1, D), qkv_spatial, preferred_element_type=jnp.float32)
    proj_one = proj_one.astype(jnp.bfloat16).reshape(FRAMES, PATCHES, 3 * D)
    spatial = lax.map(attend_sequence, proj_one)
    update = jnp.dot(spatial.reshape(-1, D), out_spatial, preferred_element_type=jnp.float32)
    middle = (frames_in.astype(jnp.float32) + update.reshape(FRAMES, PATCHES, D)).astype(jnp.bfloat16)
    second = normalize(middle)
    proj_two = jnp.dot(second.reshape(-1, D), qkv_temporal, preferred_element_type=jnp.float32)
    proj_two = proj_two.astype(jnp.bfloat16).reshape(FRAMES, PATCHES, 3 * D)
    temporal = lax.map(attend_sequence, jnp.swapaxes(proj_two, 0, 1))
    temporal = jnp.swapaxes(temporal, 0, 1)
    change = jnp.dot(temporal.reshape(-1, D), out_temporal, preferred_element_type=jnp.float32)
    return (middle.astype(jnp.float32) + change.reshape(FRAMES, PATCHES, D)).astype(jnp.bfloat16)
```

```python
import functools

import jax
import jax.numpy as jnp
from jax import lax
from jax.experimental import pallas as pl
from jax.experimental.pallas import tpu as pltpu
from jax.sharding import PartitionSpec as P

HEADS = 12
HEAD_DIM = 64
LANES = 128
TILE = 16
HALF = TILE // 2
BF16 = jnp.bfloat16
F32 = jnp.float32
VMEM = pl.BlockSpec(memory_space=pltpu.VMEM)
SMEM = pl.BlockSpec(memory_space=pltpu.SMEM)

OUTER = (0, 8, 12, 4)
INNER = (0, 1, 2, 3)


def normalize(floats):
    average = jnp.mean(floats, axis=-1, keepdims=True)
    centred = floats - average
    spread = jnp.mean(centred * centred, axis=-1, keepdims=True)
    return (centred * lax.rsqrt(spread + 1e-06)).astype(BF16)


def project(flat_rows, matrix):
    return jnp.dot(flat_rows, matrix, preferred_element_type=F32)


def attend(projected, score_form, mix_form):
    leading = projected.shape[:-1]
    split = projected.reshape(leading + (3, HEADS, HEAD_DIM))
    queries = split[..., 0, :, :]
    key_part = split[..., 1, :, :]
    values = split[..., 2, :, :]
    scores = jnp.einsum(
        score_form, queries, key_part, preferred_element_type=F32
    ) * HEAD_DIM ** (-0.5)
    weights = jax.nn.softmax(scores, axis=-1).astype(BF16)
    mixed = jnp.einsum(mix_form, weights, values, preferred_element_type=F32)
    return mixed.reshape(leading + (HEADS * HEAD_DIM,)).astype(BF16)


def attend_time(received):
    frame_total, single, item_count, columns = received.shape
    sequences = received.reshape(frame_total, item_count, columns)
    result = attend(sequences, "qbhd,kbhd->bhqk", "bhqk,kbhd->qbhd")
    return result.reshape(frame_total, single, item_count, HEADS * HEAD_DIM)


def plain_shards(frames_in, qkv_spatial, out_spatial, qkv_temporal, out_temporal):
    frame_count, patch_count, features = frames_in.shape
    wide_count = lax.axis_size("wide")
    per_group = patch_count // wide_count
    first = normalize(frames_in.astype(F32))
    proj_one = project(first.reshape(-1, features), qkv_spatial).astype(BF16)
    proj_one = proj_one.reshape(frame_count, patch_count, 3 * features)
    spatial = attend(proj_one, "bqhd,bkhd->bhqk", "bhqk,bkhd->bqhd")
    update = project(spatial.reshape(-1, features), out_spatial).reshape(
        frame_count, patch_count, features
    )
    middle = (frames_in.astype(F32) + update).astype(BF16)
    second = normalize(middle.astype(F32))
    grouped = second.reshape(frame_count, wide_count, per_group, features)
    received = lax.all_to_all(grouped, "wide", split_axis=1, concat_axis=0, tiled=True)
    frame_total, single, item_count, columns = received.shape
    local_proj = project(received.reshape(-1, columns), qkv_temporal).astype(BF16)
    local_proj = local_proj.reshape(frame_total, single, item_count, 3 * columns)
    temporal = attend_time(local_proj)
    returned = lax.all_to_all(temporal, "wide", split_axis=0, concat_axis=1, tiled=True)
    change = project(returned.reshape(-1, features), out_temporal).reshape(
        frame_count, patch_count, features
    )
    return (middle.astype(F32) + change).astype(BF16)


def attend_pair(q, k, v, length):
    rows = q.shape[0]
    low = lax.broadcasted_iota(jnp.int32, (rows, LANES), 1) < HEAD_DIM
    mixed = []
    for half in range(2):
        mine = low if half == 0 else ~low
        one = jnp.where(mine, q, jnp.zeros_like(q))
        scores = lax.dot_general(
            one, k, (((1,), (1,)), ((), ())), preferred_element_type=F32
        )
        if rows > length:
            own = lax.broadcasted_iota(
                jnp.int32, (rows, rows), 0
            ) // length == lax.broadcasted_iota(jnp.int32, (rows, rows), 1) // length
            scores = jnp.where(own, scores, -jnp.inf)
        top = jnp.max(scores, axis=-1, keepdims=True)
        weights = jnp.exp(scores - top).astype(BF16)
        values = jnp.where(mine, v, jnp.ones_like(v))
        mixed.append(jnp.dot(weights, values, preferred_element_type=F32))
    total = pltpu.roll(jnp.where(low, mixed[1], mixed[0]), HEAD_DIM, 1)
    return (jnp.where(low, mixed[0], mixed[1]) / total).astype(BF16)


def layer_rows(a_ref, wqkv, qkv, mixed, length, block):
    rows, d = a_ref.shape
    group = 256
    for j in range(3 * d // group):
        cols = slice(j * group, (j + 1) * group)
        part = jnp.dot(a_ref[...], wqkv[:, cols], preferred_element_type=F32)
        part = part.astype(BF16)
        if j < d // group:
            part = part * BF16(HEAD_DIM**-0.5)
        qkv[:, cols] = part
    for start in range(0, rows, block):
        r = slice(start, start + block)
        for c in range(0, d, LANES):
            mixed[r, c : c + LANES] = attend_pair(
                qkv[r, c : c + LANES],
                qkv[r, d + c : d + c + LANES],
                qkv[r, 2 * d + c : 2 * d + c + LANES],
                length,
            )


def spatial_kernel(outer_first, me, x, wqkv, wo, middle, o0, o1, o2, o3, a, qkv, mixed, second):
    frames, patches, d = x.shape
    outs = (o0, o1, o2, o3)
    number = me[0]
    for f in range(frames):
        a[f * patches : (f + 1) * patches, :] = normalize(x[f].astype(F32))
    layer_rows(a, wqkv, qkv, mixed, patches, patches)
    for f in range(frames):
        r = slice(f * patches, (f + 1) * patches)
        update = jnp.dot(mixed[r, :], wo[...], preferred_element_type=F32)
        mid = (x[f].astype(F32) + update).astype(BF16)
        middle[f] = mid
        second[...] = normalize(mid.astype(F32))
        for p in range(4):
            for i in range(4):
                owner = number ^ (OUTER[p] ^ INNER[i])
                rows = second[pl.ds(pl.multiple_of(owner * TILE, TILE), TILE), :]
                if outer_first:
                    outs[p][f, i] = rows
                else:
                    outs[i][f, p] = rows


def spatial(me, x, wqkv, wo, outer_first):
    frames, patches, d = x.shape
    rows = frames * patches
    block = jax.ShapeDtypeStruct((frames, 4, TILE, d), BF16)
    return pl.pallas_call(
        functools.partial(spatial_kernel, outer_first),
        in_specs=[SMEM, VMEM, VMEM, VMEM],
        out_specs=[VMEM] * 5,
        out_shape=[jax.ShapeDtypeStruct(x.shape, BF16)] + [block] * 4,
        scratch_shapes=[
            pltpu.VMEM((rows, d), BF16),
            pltpu.VMEM((rows, 3 * d), BF16),
            pltpu.VMEM((rows, d), BF16),
            pltpu.VMEM((patches, d), BF16),
        ],
        compiler_params=pltpu.CompilerParams(vmem_limit_bytes=32 << 20),
        cost_estimate=pl.CostEstimate(
            flops=8 * rows * d * d + 16 * rows * patches * d,
            bytes_accessed=8 * d * d,
            transcendentals=rows * patches * HEADS,
        ),
        name="spatial_outer" if outer_first else "spatial_inner",
    )(me, x, wqkv, wo)


def regroup_kernel(*refs):
    ins, outs = refs[:4], refs[4:]
    for b in range(4):
        for a in range(4):
            if len(ins[0].shape) == 4:
                outs[b][a] = ins[a][:, b]
            else:
                outs[b][a] = ins[a][b]


def regroup(pieces):
    shape = pieces[0].shape
    shape = (4, shape[0]) + shape[2:] if len(shape) == 4 else shape
    return pl.pallas_call(
        regroup_kernel,
        in_specs=[VMEM] * 4,
        out_specs=[VMEM] * 4,
        out_shape=[jax.ShapeDtypeStruct(shape, BF16)] * 4,
        cost_estimate=pl.CostEstimate(flops=0, bytes_accessed=1 << 20, transcendentals=0),
        name="regroup",
    )(*pieces)


def chosen(rows, columns, source):
    r = lax.broadcasted_iota(jnp.int32, (rows, columns), 0)
    c = lax.broadcasted_iota(jnp.int32, (rows, columns), 1)
    return (c == source(r)).astype(F32).astype(BF16)


def temporal_kernel(half, outer_first, *refs):
    z_parts, y_parts = refs[:4], refs[4:8]
    wqkv, wo = refs[8:10]
    outs = refs[10:14]
    gathered, a, qkv, mixed = refs[14:]
    d = a.shape[1]
    length = a.shape[0] // HALF
    pick = chosen(HALF * TILE, TILE * TILE, lambda r: (r % TILE) * TILE + half * HALF + r // TILE)
    for p in range(4):
        for i in range(4):
            base = i * 4 * TILE
            for f in range(2):
                gathered[base + f * TILE : base + (f + 1) * TILE, :] = z_parts[i][p, f]
                gathered[base + (f + 2) * TILE : base + (f + 3) * TILE, :] = y_parts[p][i, f]
        taken = jnp.dot(pick, gathered[...], preferred_element_type=F32).astype(BF16)
        for q in range(HALF):
            start = q * length + p * TILE
            a[start : start + TILE, :] = taken[q * TILE : (q + 1) * TILE]
    layer_rows(a, wqkv, qkv, mixed, length, 4 * length)
    back = chosen(HALF * TILE, HALF * TILE, lambda r: (r % HALF) * TILE + r // HALF)
    for p in range(4):
        rows = jnp.concatenate(
            [mixed[q * length + p * TILE : q * length + (p + 1) * TILE, :] for q in range(HALF)],
            axis=0,
        )
        change = jnp.dot(rows, wo[...], preferred_element_type=F32).astype(BF16)
        change = jnp.dot(back, change, preferred_element_type=F32).astype(BF16)
        for i in range(4):
            piece = change[i * 2 * TILE : (i + 1) * 2 * TILE]
            if outer_first:
                outs[p][i] = piece
            else:
                outs[i][p] = piece


def temporal(half, z_parts, y_parts, wqkv, wo, outer_first):
    d = wo.shape[0]
    length = 4 * TILE
    rows = HALF * length
    block = jax.ShapeDtypeStruct((4, 2 * TILE, d), BF16)
    return pl.pallas_call(
        functools.partial(temporal_kernel, half, outer_first),
        in_specs=[VMEM] * 10,
        out_specs=[VMEM] * 4,
        out_shape=[block] * 4,
        scratch_shapes=[
            pltpu.VMEM((TILE * TILE, d), BF16),
            pltpu.VMEM((rows, d), BF16),
            pltpu.VMEM((rows, 3 * d), BF16),
            pltpu.VMEM((rows, d), BF16),
        ],
        compiler_params=pltpu.CompilerParams(vmem_limit_bytes=32 << 20),
        cost_estimate=pl.CostEstimate(
            flops=8 * rows * d * d + 16 * rows * 4 * length * d,
            bytes_accessed=8 * d * d,
            transcendentals=rows * 4 * length * HEADS,
        ),
        name="temporal",
    )(*z_parts, *y_parts, wqkv, wo)


def last_kernel(me, mid01, mid23, *refs):
    early, late, out = refs[:4], refs[4:8], refs[8]
    number = me[0]
    f = pl.program_id(0)

    def add(mid, frame, at):
        for p in range(4):
            for i in range(4):
                owner = number ^ (OUTER[p] ^ INNER[i])
                rows = pl.ds(pl.multiple_of(owner * TILE, TILE), TILE)
                change = jnp.concatenate(
                    [
                        early[i][p].astype(F32)[at * HALF : (at + 1) * HALF],
                        late[p][i].astype(F32)[at * HALF : (at + 1) * HALF],
                    ],
                    axis=0,
                )
                out[0, rows, :] = (mid[frame, rows, :].astype(F32) + change).astype(BF16)

    for at in range(4):
        pl.when(f == at)(functools.partial(add, mid01 if at < 2 else mid23, at % 2, at))


def last(me, mid01, mid23, early, late):
    _, patches, d = mid01.shape
    return pl.pallas_call(
        last_kernel,
        grid=(4,),
        in_specs=[SMEM] + [VMEM] * 10,
        out_specs=pl.BlockSpec((1, patches, d), lambda f: (f, 0, 0)),
        out_shape=jax.ShapeDtypeStruct((4, patches, d), BF16),
        cost_estimate=pl.CostEstimate(
            flops=patches * d * 4, bytes_accessed=patches * d * 8, transcendentals=0
        ),
        name="last",
    )(me, mid01, mid23, *early, *late)


def exchange(pieces, masks):
    size = lax.axis_size("wide")
    return [pieces[0]] + [
        lax.ppermute(piece, "wide", [(w, w ^ mask) for w in range(size)])
        for piece, mask in zip(pieces[1:], masks[1:])
    ]


def shards(frames_in, qkv_spatial, out_spatial, qkv_temporal, out_temporal):
    me = lax.axis_index("wide").astype(jnp.int32).reshape(1)
    mid01, *pieces = spatial(me, frames_in[:2], qkv_spatial, out_spatial, True)
    z_parts = exchange(regroup(exchange(pieces, OUTER)), INNER)
    mid23, *pieces = spatial(me, frames_in[2:], qkv_spatial, out_spatial, False)
    y_parts = exchange(regroup(exchange(pieces, INNER)), OUTER)
    pieces = temporal(0, z_parts, y_parts, qkv_temporal, out_temporal, True)
    early = exchange(regroup(exchange(pieces, OUTER)), INNER)
    pieces = temporal(1, z_parts, y_parts, qkv_temporal, out_temporal, False)
    late = exchange(regroup(exchange(pieces, INNER)), OUTER)
    return last(me, mid01, mid23, early, late)


def solution(mesh):
    wide = mesh.shape["wide"]

    def whole(frames_in, *weights):
        local = frames_in.shape[0] // (wide * mesh.shape["groups"])
        fits = wide == 16 and local == 4 and frames_in.shape[1] == wide * TILE
        return jax.shard_map(
            shards if fits else plain_shards,
            mesh=mesh,
            in_specs=(P(("groups", "wide"), None, None), P(), P(), P(), P()),
            out_specs=P(("groups", "wide"), None, None),
            check_vma=False,
        )(frames_in, *weights)

    return whole
```

```python
import functools

import jax
import jax.numpy as jnp
from jax import lax
from jax.experimental import pallas as pl
from jax.experimental.pallas import tpu as pltpu
from jax.sharding import PartitionSpec as P

HEADS = 12
HEAD_DIM = 64
LANES = 128
TILE = 16
HALF = TILE // 2
BF16 = jnp.bfloat16
F32 = jnp.float32
VMEM = pl.BlockSpec(memory_space=pltpu.VMEM)
SMEM = pl.BlockSpec(memory_space=pltpu.SMEM)
HBM = pl.BlockSpec(memory_space=pltpu.HBM)

OUTER = (0, 8, 12, 4)
INNER = (0, 1, 2, 3)


def normalize(floats):
    average = jnp.mean(floats, axis=-1, keepdims=True)
    centred = floats - average
    spread = jnp.mean(centred * centred, axis=-1, keepdims=True)
    return (centred * lax.rsqrt(spread + 1e-06)).astype(BF16)


def project(flat_rows, matrix):
    return jnp.dot(flat_rows, matrix, preferred_element_type=F32)


def attend(projected, score_form, mix_form):
    leading = projected.shape[:-1]
    split = projected.reshape(leading + (3, HEADS, HEAD_DIM))
    queries = split[..., 0, :, :]
    key_part = split[..., 1, :, :]
    values = split[..., 2, :, :]
    scores = jnp.einsum(
        score_form, queries, key_part, preferred_element_type=F32
    ) * HEAD_DIM ** (-0.5)
    weights = jax.nn.softmax(scores, axis=-1).astype(BF16)
    mixed = jnp.einsum(mix_form, weights, values, preferred_element_type=F32)
    return mixed.reshape(leading + (HEADS * HEAD_DIM,)).astype(BF16)


def attend_time(received):
    frame_total, single, item_count, columns = received.shape
    sequences = received.reshape(frame_total, item_count, columns)
    result = attend(sequences, "qbhd,kbhd->bhqk", "bhqk,kbhd->qbhd")
    return result.reshape(frame_total, single, item_count, HEADS * HEAD_DIM)


def plain_shards(frames_in, qkv_spatial, out_spatial, qkv_temporal, out_temporal):
    frame_count, patch_count, features = frames_in.shape
    wide_count = lax.axis_size("wide")
    per_group = patch_count // wide_count
    first = normalize(frames_in.astype(F32))
    proj_one = project(first.reshape(-1, features), qkv_spatial).astype(BF16)
    proj_one = proj_one.reshape(frame_count, patch_count, 3 * features)
    spatial = attend(proj_one, "bqhd,bkhd->bhqk", "bhqk,bkhd->bqhd")
    update = project(spatial.reshape(-1, features), out_spatial).reshape(
        frame_count, patch_count, features
    )
    middle = (frames_in.astype(F32) + update).astype(BF16)
    second = normalize(middle.astype(F32))
    grouped = second.reshape(frame_count, wide_count, per_group, features)
    received = lax.all_to_all(grouped, "wide", split_axis=1, concat_axis=0, tiled=True)
    frame_total, single, item_count, columns = received.shape
    local_proj = project(received.reshape(-1, columns), qkv_temporal).astype(BF16)
    local_proj = local_proj.reshape(frame_total, single, item_count, 3 * columns)
    temporal = attend_time(local_proj)
    returned = lax.all_to_all(temporal, "wide", split_axis=0, concat_axis=1, tiled=True)
    change = project(returned.reshape(-1, features), out_temporal).reshape(
        frame_count, patch_count, features
    )
    return (middle.astype(F32) + change).astype(BF16)


def attend_pair(q, k, v, length):
    rows = q.shape[0]
    low = lax.broadcasted_iota(jnp.int32, (rows, LANES), 1) < HEAD_DIM
    mixed = []
    for half in range(2):
        mine = low if half == 0 else ~low
        one = jnp.where(mine, q, jnp.zeros_like(q))
        scores = lax.dot_general(
            one, k, (((1,), (1,)), ((), ())), preferred_element_type=F32
        )
        if rows > length:
            own = lax.broadcasted_iota(
                jnp.int32, (rows, rows), 0
            ) // length == lax.broadcasted_iota(jnp.int32, (rows, rows), 1) // length
            scores = jnp.where(own, scores, -jnp.inf)
        top = jnp.max(scores, axis=-1, keepdims=True)
        weights = jnp.exp(scores - top).astype(BF16)
        values = jnp.where(mine, v, jnp.ones_like(v))
        mixed.append(jnp.dot(weights, values, preferred_element_type=F32))
    total = pltpu.roll(jnp.where(low, mixed[1], mixed[0]), HEAD_DIM, 1)
    return (jnp.where(low, mixed[0], mixed[1]) / total).astype(BF16)


def layer_rows(a_ref, wqkv, qkv, mixed, length, block):
    rows, d = a_ref.shape
    group = 256
    for j in range(3 * d // group):
        cols = slice(j * group, (j + 1) * group)
        part = jnp.dot(a_ref[...], wqkv[:, cols], preferred_element_type=F32)
        part = part.astype(BF16)
        if j < d // group:
            part = part * BF16(HEAD_DIM**-0.5)
        qkv[:, cols] = part
    for start in range(0, rows, block):
        r = slice(start, start + block)
        for c in range(0, d, LANES):
            mixed[r, c : c + LANES] = attend_pair(
                qkv[r, c : c + LANES],
                qkv[r, d + c : d + c + LANES],
                qkv[r, 2 * d + c : 2 * d + c + LANES],
                length,
            )


def spatial_kernel(outer_first, begin, me, x_in, wqkv_in, wo_in, middle, o0, o1, o2, o3, x, a, qkv, mixed, second, sems, *held):
    frames, patches, d = x.shape
    outs = (o0, o1, o2, o3)
    number = me[0]
    x_copies = [pltpu.make_async_copy(x_in.at[begin + f], x.at[f], sems.at[f]) for f in range(frames)]
    for copy in x_copies:
        copy.start()
    wqkv, wo = wqkv_in, wo_in
    if held:
        wqkv, wo = held
        parts = [pl.ds(c, 192) for c in range(0, d, 192)]
        copies = [
            pltpu.make_async_copy(wqkv_in.at[c], wqkv.at[c], sems.at[frames + j])
            for j, c in enumerate(parts)
        ]
        wo_copy = pltpu.make_async_copy(wo_in, wo, sems.at[frames + len(copies)])
        for copy in copies:
            copy.start()
        wo_copy.start()
    for f in range(frames):
        x_copies[f].wait()
        a[f * patches : (f + 1) * patches, :] = normalize(x[f].astype(F32))
    if held:
        for copy in copies:
            copy.wait()
    layer_rows(a, wqkv, qkv, mixed, patches, patches)
    if held:
        wo_copy.wait()
    for f in range(frames):
        r = slice(f * patches, (f + 1) * patches)
        update = jnp.dot(mixed[r, :], wo[...], preferred_element_type=F32)
        mid = (x[f].astype(F32) + update).astype(BF16)
        middle[f] = mid
        second[...] = normalize(mid.astype(F32))
        for p in range(4):
            for i in range(4):
                owner = number ^ (OUTER[p] ^ INNER[i])
                rows = second[pl.ds(pl.multiple_of(owner * TILE, TILE), TILE), :]
                if outer_first:
                    outs[p][f, i] = rows
                else:
                    outs[i][f, p] = rows


def spatial(me, x, begin, frames, wqkv, wo, outer_first, fetch):
    _, patches, d = x.shape
    rows = frames * patches
    block = jax.ShapeDtypeStruct((frames, 4, TILE, d), BF16)
    return pl.pallas_call(
        functools.partial(spatial_kernel, outer_first, begin),
        in_specs=[SMEM, HBM] + [HBM if fetch else VMEM] * 2,
        out_specs=[VMEM] * 5,
        out_shape=[jax.ShapeDtypeStruct((frames, patches, d), BF16)] + [block] * 4,
        scratch_shapes=[
            pltpu.VMEM((frames, patches, d), BF16),
            pltpu.VMEM((rows, d), BF16),
            pltpu.VMEM((rows, 3 * d), BF16),
            pltpu.VMEM((rows, d), BF16),
            pltpu.VMEM((patches, d), BF16),
            pltpu.SemaphoreType.DMA((frames + 3 * d // 256 + 1,)),
        ]
        + ([pltpu.VMEM(wqkv.shape, BF16), pltpu.VMEM(wo.shape, BF16)] if fetch else []),
        compiler_params=pltpu.CompilerParams(vmem_limit_bytes=(58 if fetch else 32) << 20),
        cost_estimate=pl.CostEstimate(
            flops=8 * rows * d * d + 16 * rows * patches * d,
            bytes_accessed=8 * d * d,
            transcendentals=rows * patches * HEADS,
        ),
        name="spatial_outer" if outer_first else "spatial_inner",
    )(me, x, wqkv, wo)


def regroup_kernel(*refs):
    ins, outs = refs[:4], refs[4:]
    for b in range(4):
        for a in range(4):
            if len(ins[0].shape) == 4:
                outs[b][a] = ins[a][:, b]
            else:
                outs[b][a] = ins[a][b]


def regroup(pieces):
    shape = pieces[0].shape
    shape = (4, shape[0]) + shape[2:] if len(shape) == 4 else shape
    return pl.pallas_call(
        regroup_kernel,
        in_specs=[VMEM] * 4,
        out_specs=[VMEM] * 4,
        out_shape=[jax.ShapeDtypeStruct(shape, BF16)] * 4,
        compiler_params=pltpu.CompilerParams(vmem_limit_bytes=4 << 20),
        cost_estimate=pl.CostEstimate(flops=0, bytes_accessed=1 << 20, transcendentals=0),
        name="regroup",
    )(*pieces)


def chosen(rows, columns, source):
    r = lax.broadcasted_iota(jnp.int32, (rows, columns), 0)
    c = lax.broadcasted_iota(jnp.int32, (rows, columns), 1)
    return (c == source(r)).astype(F32).astype(BF16)


def temporal_kernel(half, outer_first, *refs):
    z_parts, y_parts = refs[:4], refs[4:8]
    wqkv, wo = refs[8:10]
    outs = refs[10:14]
    gathered, a, qkv, mixed = refs[14:]
    d = a.shape[1]
    length = a.shape[0] // HALF
    pick = chosen(HALF * TILE, TILE * TILE, lambda r: (r % TILE) * TILE + half * HALF + r // TILE)
    for p in range(4):
        for i in range(4):
            base = i * 4 * TILE
            for f in range(2):
                gathered[base + f * TILE : base + (f + 1) * TILE, :] = z_parts[i][p, f]
                gathered[base + (f + 2) * TILE : base + (f + 3) * TILE, :] = y_parts[p][i, f]
        taken = jnp.dot(pick, gathered[...], preferred_element_type=F32).astype(BF16)
        for q in range(HALF):
            start = q * length + p * TILE
            a[start : start + TILE, :] = taken[q * TILE : (q + 1) * TILE]
    layer_rows(a, wqkv, qkv, mixed, length, 4 * length)
    back = chosen(HALF * TILE, HALF * TILE, lambda r: (r % HALF) * TILE + r // HALF)
    for p in range(4):
        rows = jnp.concatenate(
            [mixed[q * length + p * TILE : q * length + (p + 1) * TILE, :] for q in range(HALF)],
            axis=0,
        )
        change = jnp.dot(rows, wo[...], preferred_element_type=F32).astype(BF16)
        change = jnp.dot(back, change, preferred_element_type=F32).astype(BF16)
        for i in range(4):
            piece = change[i * 2 * TILE : (i + 1) * 2 * TILE]
            if outer_first:
                outs[p][i] = piece
            else:
                outs[i][p] = piece


def temporal(half, z_parts, y_parts, wqkv, wo, outer_first):
    d = wo.shape[0]
    length = 4 * TILE
    rows = HALF * length
    block = jax.ShapeDtypeStruct((4, 2 * TILE, d), BF16)
    return pl.pallas_call(
        functools.partial(temporal_kernel, half, outer_first),
        in_specs=[VMEM] * 10,
        out_specs=[VMEM] * 4,
        out_shape=[block] * 4,
        scratch_shapes=[
            pltpu.VMEM((TILE * TILE, d), BF16),
            pltpu.VMEM((rows, d), BF16),
            pltpu.VMEM((rows, 3 * d), BF16),
            pltpu.VMEM((rows, d), BF16),
        ],
        compiler_params=pltpu.CompilerParams(vmem_limit_bytes=32 << 20),
        cost_estimate=pl.CostEstimate(
            flops=8 * rows * d * d + 16 * rows * 4 * length * d,
            bytes_accessed=8 * d * d,
            transcendentals=rows * 4 * length * HEADS,
        ),
        name="temporal",
    )(*z_parts, *y_parts, wqkv, wo)


def last_kernel(me, mid01, mid23, *refs):
    early, late, out = refs[:4], refs[4:8], refs[8]
    number = me[0]
    f = pl.program_id(0)

    def add(mid, frame, at):
        for p in range(4):
            for i in range(4):
                owner = number ^ (OUTER[p] ^ INNER[i])
                rows = pl.ds(pl.multiple_of(owner * TILE, TILE), TILE)
                change = jnp.concatenate(
                    [
                        early[i][p].astype(F32)[at * HALF : (at + 1) * HALF],
                        late[p][i].astype(F32)[at * HALF : (at + 1) * HALF],
                    ],
                    axis=0,
                )
                out[0, rows, :] = (mid[frame, rows, :].astype(F32) + change).astype(BF16)

    for at in range(4):
        pl.when(f == at)(functools.partial(add, mid01 if at < 2 else mid23, at % 2, at))


def last(me, mid01, mid23, early, late):
    _, patches, d = mid01.shape
    return pl.pallas_call(
        last_kernel,
        grid=(4,),
        in_specs=[SMEM] + [VMEM] * 10,
        out_specs=pl.BlockSpec((1, patches, d), lambda f: (f, 0, 0)),
        out_shape=jax.ShapeDtypeStruct((4, patches, d), BF16),
        compiler_params=pltpu.CompilerParams(vmem_limit_bytes=16 << 20),
        cost_estimate=pl.CostEstimate(
            flops=patches * d * 4, bytes_accessed=patches * d * 8, transcendentals=0
        ),
        name="last",
    )(me, mid01, mid23, *early, *late)


def exchange(pieces, masks):
    size = lax.axis_size("wide")
    return [pieces[0]] + [
        lax.ppermute(piece, "wide", [(w, w ^ mask) for w in range(size)])
        for piece, mask in zip(pieces[1:], masks[1:])
    ]


def shards(frames_in, qkv_spatial, out_spatial, qkv_temporal, out_temporal):
    me = lax.axis_index("wide").astype(jnp.int32).reshape(1)
    mid01, *pieces = spatial(me, frames_in, 0, 2, qkv_spatial, out_spatial, True, True)
    z_parts = exchange(regroup(exchange(pieces, OUTER)), INNER)
    mid23, *pieces = spatial(me, frames_in, 2, 2, qkv_spatial, out_spatial, False, False)
    y_parts = exchange(regroup(exchange(pieces, INNER)), OUTER)
    pieces = temporal(0, z_parts, y_parts, qkv_temporal, out_temporal, True)
    early = exchange(regroup(exchange(pieces, OUTER)), INNER)
    pieces = temporal(1, z_parts, y_parts, qkv_temporal, out_temporal, False)
    late = exchange(regroup(exchange(pieces, INNER)), OUTER)
    return last(me, mid01, mid23, early, late)


def solution(mesh):
    wide = mesh.shape["wide"]

    def whole(frames_in, *weights):
        local = frames_in.shape[0] // (wide * mesh.shape["groups"])
        fits = wide == 16 and local == 4 and frames_in.shape[1] == wide * TILE
        return jax.shard_map(
            shards if fits else plain_shards,
            mesh=mesh,
            in_specs=(P(("groups", "wide"), None, None), P(), P(), P(), P()),
            out_specs=P(("groups", "wide"), None, None),
            check_vma=False,
        )(frames_in, *weights)

    return whole
```

```python
import functools

import jax
import jax.numpy as jnp
from jax import lax
from jax.experimental import pallas as pl
from jax.experimental.pallas import tpu as pltpu
from jax.sharding import PartitionSpec as P

HEADS = 12
HEAD_DIM = 64
LANES = 128
TILE = 16
HALF = TILE // 2
GROUP = 256
LAG = 1
BF16 = jnp.bfloat16
F32 = jnp.float32
VMEM = pl.BlockSpec(memory_space=pltpu.VMEM)
SMEM = pl.BlockSpec(memory_space=pltpu.SMEM)
HBM = pl.BlockSpec(memory_space=pltpu.HBM)

OUTER = (0, 8, 12, 4)
INNER = (0, 1, 2, 3)


def normalize(floats):
    average = jnp.mean(floats, axis=-1, keepdims=True)
    centred = floats - average
    spread = jnp.mean(centred * centred, axis=-1, keepdims=True)
    return (centred * lax.rsqrt(spread + 1e-06)).astype(BF16)


def project(flat_rows, matrix):
    return jnp.dot(flat_rows, matrix, preferred_element_type=F32)


def plain_attend(projected, score_form, mix_form):
    leading = projected.shape[:-1]
    split = projected.reshape(leading + (3, HEADS, HEAD_DIM))
    queries = split[..., 0, :, :]
    key_part = split[..., 1, :, :]
    values = split[..., 2, :, :]
    scores = jnp.einsum(
        score_form, queries, key_part, preferred_element_type=F32
    ) * HEAD_DIM ** (-0.5)
    weights = jax.nn.softmax(scores, axis=-1).astype(BF16)
    mixed = jnp.einsum(mix_form, weights, values, preferred_element_type=F32)
    return mixed.reshape(leading + (HEADS * HEAD_DIM,)).astype(BF16)


def attend_time(received):
    frame_total, single, item_count, columns = received.shape
    sequences = received.reshape(frame_total, item_count, columns)
    result = plain_attend(sequences, "qbhd,kbhd->bhqk", "bhqk,kbhd->qbhd")
    return result.reshape(frame_total, single, item_count, HEADS * HEAD_DIM)


def plain_shards(frames_in, qkv_spatial, out_spatial, qkv_temporal, out_temporal):
    frame_count, patch_count, features = frames_in.shape
    wide_count = lax.axis_size("wide")
    per_group = patch_count // wide_count
    first = normalize(frames_in.astype(F32))
    proj_one = project(first.reshape(-1, features), qkv_spatial).astype(BF16)
    proj_one = proj_one.reshape(frame_count, patch_count, 3 * features)
    spatial = plain_attend(proj_one, "bqhd,bkhd->bhqk", "bhqk,bkhd->bqhd")
    update = project(spatial.reshape(-1, features), out_spatial).reshape(
        frame_count, patch_count, features
    )
    middle = (frames_in.astype(F32) + update).astype(BF16)
    second = normalize(middle.astype(F32))
    grouped = second.reshape(frame_count, wide_count, per_group, features)
    received = lax.all_to_all(grouped, "wide", split_axis=1, concat_axis=0, tiled=True)
    frame_total, single, item_count, columns = received.shape
    local_proj = project(received.reshape(-1, columns), qkv_temporal).astype(BF16)
    local_proj = local_proj.reshape(frame_total, single, item_count, 3 * columns)
    temporal = attend_time(local_proj)
    returned = lax.all_to_all(temporal, "wide", split_axis=0, concat_axis=1, tiled=True)
    change = project(returned.reshape(-1, features), out_temporal).reshape(
        frame_count, patch_count, features
    )
    return (middle.astype(F32) + change).astype(BF16)


def project_rows(a, wqkv, qkv, places, j):
    d = a.shape[1]
    for start in range(j * d, (j + 1) * d, GROUP):
        cols = slice(start, start + GROUP)
        part = jnp.dot(a[...], wqkv[:, cols], preferred_element_type=F32).astype(BF16)
        part = part * BF16(HEAD_DIM**-0.5) if j == 0 else part
        size = a.shape[0] // len(places)
        for n, place in enumerate(places):
            qkv[place : place + size, cols] = part[n * size : (n + 1) * size]


def attend(qkv, mixed, blocks, bias=None):
    d = mixed.shape[1]
    units = [(r, c, half) for r in blocks for c in range(0, d, LANES) for half in range(2)]
    size = blocks[0].stop - blocks[0].start
    low = lax.broadcasted_iota(jnp.int32, (size, LANES), 1) < HEAD_DIM
    begun, sums = {}, {}

    def begin(n):
        r, c, half = units[n]
        q = qkv[r, c : c + LANES]
        one = jnp.where(low if half == 0 else ~low, q, jnp.zeros_like(q))
        scores = lax.dot_general(
            one,
            qkv[r, d + c : d + c + LANES],
            (((1,), (1,)), ((), ())),
            preferred_element_type=F32,
        )
        if bias is not None:
            scores = scores + bias[...]
        begun[n] = scores, jnp.max(scores, axis=-1, keepdims=True)

    def end(n):
        r, c, half = units[n]
        scores, top = begun.pop(n)
        weights = jnp.exp(scores - top).astype(BF16)
        v = qkv[r, 2 * d + c : 2 * d + c + LANES]
        values = jnp.where(low if half == 0 else ~low, v, jnp.ones_like(v))
        sums[half] = jnp.dot(weights, values, preferred_element_type=F32)
        if half == 1:
            total = pltpu.roll(jnp.where(low, sums[1], sums[0]), HEAD_DIM, 1)
            mixed[r, c : c + LANES] = (jnp.where(low, sums[0], sums[1]) / total).astype(BF16)

    for n in range(len(units) + LAG):
        if n < len(units):
            begin(n)
        if n >= LAG:
            end(n - LAG)


def spatial_kernel(outer_first, begin, fetch, me, x_in, wqkv_in, wo_in, middle, *refs):
    frames, patches, d = middle.shape
    outs, (a, qkv, mixed, second, *held) = refs[:4], refs[4:]
    number = me[0]
    if fetch:
        x, wqkv, wo, sems = held
        pairs = [(x_in.at[pl.ds(begin, frames)], x)]
        pairs += [(wqkv_in.at[:, pl.ds(j * d, d)], wqkv.at[:, pl.ds(j * d, d)]) for j in range(3)]
        pairs += [(wo_in, wo)]
        copies = [pltpu.make_async_copy(*pair, sems.at[n]) for n, pair in enumerate(pairs)]
        for copy in copies:
            copy.start()
        copies[0].wait()
    else:
        x, wqkv, wo = x_in.at[pl.ds(begin, frames)], wqkv_in, wo_in
    for f in range(frames):
        a[f * patches : (f + 1) * patches, :] = normalize(x[f].astype(F32))
    for j in range(3):
        if fetch:
            copies[1 + j].wait()
        project_rows(a, wqkv, qkv, (0,), j)
    if fetch:
        copies[4].wait()
    attend(qkv, mixed, [slice(f * patches, (f + 1) * patches) for f in range(frames)])
    for f in range(frames):
        r = slice(f * patches, (f + 1) * patches)
        update = jnp.dot(mixed[r, :], wo[...], preferred_element_type=F32)
        mid = (x[f].astype(F32) + update).astype(BF16)
        middle[f] = mid
        second[...] = normalize(mid.astype(F32))
        for p in range(4):
            for i in range(4):
                owner = number ^ (OUTER[p] ^ INNER[i])
                rows = second[pl.ds(pl.multiple_of(owner * TILE, TILE), TILE), :]
                if outer_first:
                    outs[p][f, i] = rows
                else:
                    outs[i][f, p] = rows


def spatial(me, x, begin, frames, wqkv, wo, outer_first, fetch):
    _, patches, d = x.shape
    rows = frames * patches
    block = jax.ShapeDtypeStruct((frames, 4, TILE, d), BF16)
    held = [
        pltpu.VMEM((frames, patches, d), BF16),
        pltpu.VMEM(wqkv.shape, BF16),
        pltpu.VMEM(wo.shape, BF16),
        pltpu.SemaphoreType.DMA((5,)),
    ]
    return pl.pallas_call(
        functools.partial(spatial_kernel, outer_first, begin, fetch),
        in_specs=[SMEM] + [HBM if fetch else VMEM] * 3,
        out_specs=[VMEM] * 5,
        out_shape=[jax.ShapeDtypeStruct((frames, patches, d), BF16)] + [block] * 4,
        scratch_shapes=[
            pltpu.VMEM((rows, d), BF16),
            pltpu.VMEM((rows, 3 * d), BF16),
            pltpu.VMEM((rows, d), BF16),
            pltpu.VMEM((patches, d), BF16),
        ]
        + (held if fetch else []),
        compiler_params=pltpu.CompilerParams(vmem_limit_bytes=(52 if fetch else 24) << 20),
        cost_estimate=pl.CostEstimate(
            flops=8 * rows * d * d + 16 * rows * patches * d,
            bytes_accessed=8 * d * d,
            transcendentals=rows * patches * HEADS,
        ),
        name="spatial_outer" if outer_first else "spatial_inner",
    )(me, x, wqkv, wo)


def regroup_kernel(*refs):
    ins, outs = refs[:4], refs[4:]
    for b in range(4):
        for a in range(4):
            if len(ins[0].shape) == 4:
                outs[b][a] = ins[a][:, b]
            else:
                outs[b][a] = ins[a][b]


def regroup(pieces):
    shape = pieces[0].shape
    shape = (4, shape[0]) + shape[2:] if len(shape) == 4 else shape
    return pl.pallas_call(
        regroup_kernel,
        in_specs=[VMEM] * 4,
        out_specs=[VMEM] * 4,
        out_shape=[jax.ShapeDtypeStruct(shape, BF16)] * 4,
        compiler_params=pltpu.CompilerParams(vmem_limit_bytes=4 << 20),
        cost_estimate=pl.CostEstimate(flops=0, bytes_accessed=1 << 20, transcendentals=0),
        name="regroup",
    )(*pieces)


def chosen(rows, columns, source):
    r = lax.broadcasted_iota(jnp.int32, (rows, columns), 0)
    c = lax.broadcasted_iota(jnp.int32, (rows, columns), 1)
    return (c == source(r)).astype(F32).astype(BF16)


def gather(parts, tile, scratch, positions, length, a):
    count = positions.stop - positions.start
    pick = chosen(
        count * TILE, TILE * TILE, lambda r: (r % TILE) * TILE + positions.start + r // TILE
    )
    for block in range(2):
        for n in range(TILE):
            p, i, f = 2 * block + n // 8, n // 2 % 4, n % 2
            scratch[n * TILE : (n + 1) * TILE, :] = tile(parts, p, i, f)
        taken = jnp.dot(pick, scratch[...], preferred_element_type=F32).astype(BF16)
        for q in range(count):
            start = q * length + block * TILE
            a[start : start + TILE, :] = taken[q * TILE : (q + 1) * TILE]


def project_kernel(*refs):
    parts, wqkv, qkv, scratch, a = refs[:4], *refs[4:]
    gather(parts, lambda z, p, i, f: z[i][p, f], scratch, slice(0, TILE), 2 * TILE, a)
    for j in range(3):
        project_rows(a, wqkv, qkv, (0,), j)


def project_early(parts, wqkv):
    d = wqkv.shape[0]
    rows = TILE * 2 * TILE
    return pl.pallas_call(
        project_kernel,
        in_specs=[VMEM] * 5,
        out_specs=VMEM,
        out_shape=jax.ShapeDtypeStruct((rows, 3 * d), BF16),
        scratch_shapes=[pltpu.VMEM((TILE * TILE, d), BF16), pltpu.VMEM((rows, d), BF16)],
        compiler_params=pltpu.CompilerParams(vmem_limit_bytes=24 << 20),
        cost_estimate=pl.CostEstimate(
            flops=6 * rows * d * d, bytes_accessed=6 * d * d, transcendentals=0
        ),
        name="project_early",
    )(*parts, wqkv)


def temporal_kernel(half, outer_first, early, *refs):
    parts, wqkv, wo, outs = refs[:4], refs[4], refs[5], refs[6:10]
    scratch, a, qkv, mixed, change, bias = refs[10:]
    length = 2 * TILE
    run = 4 * length
    row, column = (lax.broadcasted_iota(jnp.int32, bias.shape, axis) for axis in range(2))
    other = ((row ^ column) & (run - length)) != 0
    bias[...] = jnp.where(other, -jnp.inf, 0.0)
    gather(
        parts,
        lambda y, p, i, f: y[p][i, f],
        scratch,
        slice(half * HALF, (half + 1) * HALF),
        length,
        a,
    )
    groups = range(HALF // 4)
    for g in groups:
        first = (half * HALF + 4 * g) * length
        qkv[2 * g * run : (2 * g + 1) * run, :] = early[first : first + run, :]
    for j in range(3):
        project_rows(a, wqkv, qkv, [(2 * g + 1) * run for g in groups], j)
    attend(qkv, mixed, [slice(2 * g * run, 2 * (g + 1) * run) for g in groups], bias)
    change[...] = jnp.dot(mixed[...], wo[...], preferred_element_type=F32).astype(BF16)
    back = chosen(HALF * TILE, HALF * TILE, lambda r: (r % HALF) * TILE + r // HALF)
    for chunk in range(2):
        for block in range(2):
            starts = [
                (q // 4 * 2 + chunk) * run + q % 4 * length + block * TILE for q in range(HALF)
            ]
            rows = jnp.concatenate([change[start : start + TILE, :] for start in starts], axis=0)
            rows = jnp.dot(back, rows, preferred_element_type=F32).astype(BF16)
            for n in range(8):
                p, i = 2 * block + n // 4, n % 4
                tile = rows[n * TILE : (n + 1) * TILE]
                at = slice(chunk * TILE, (chunk + 1) * TILE)
                if outer_first:
                    outs[p][i, at] = tile
                else:
                    outs[i][p, at] = tile


def temporal(half, early, parts, wqkv, wo, outer_first):
    d = wo.shape[0]
    rows = HALF * 2 * TILE
    block = jax.ShapeDtypeStruct((4, 2 * TILE, d), BF16)
    return pl.pallas_call(
        functools.partial(temporal_kernel, half, outer_first),
        in_specs=[VMEM] * 7,
        out_specs=[VMEM] * 4,
        out_shape=[block] * 4,
        scratch_shapes=[
            pltpu.VMEM((TILE * TILE, d), BF16),
            pltpu.VMEM((rows, d), BF16),
            pltpu.VMEM((2 * rows, 3 * d), BF16),
            pltpu.VMEM((2 * rows, d), BF16),
            pltpu.VMEM((2 * rows, d), BF16),
            pltpu.VMEM((16 * TILE, 16 * TILE), F32),
        ],
        compiler_params=pltpu.CompilerParams(vmem_limit_bytes=24 << 20),
        cost_estimate=pl.CostEstimate(
            flops=10 * rows * d * d + 32 * rows * GROUP * d,
            bytes_accessed=8 * d * d,
            transcendentals=2 * rows * GROUP * HEADS,
        ),
        name="temporal",
    )(early, *parts, wqkv, wo)


def last_kernel(me, mid01, mid23, *refs):
    early, late, out = refs[:4], refs[4:8], refs[8]
    number = me[0]
    f = pl.program_id(0)

    def add(mid, frame, at):
        for p in range(4):
            for i in range(4):
                owner = number ^ (OUTER[p] ^ INNER[i])
                rows = pl.ds(pl.multiple_of(owner * TILE, TILE), TILE)
                change = jnp.concatenate(
                    [
                        early[i][p].astype(F32)[at * HALF : (at + 1) * HALF],
                        late[p][i].astype(F32)[at * HALF : (at + 1) * HALF],
                    ],
                    axis=0,
                )
                out[0, rows, :] = (mid[frame, rows, :].astype(F32) + change).astype(BF16)

    for at in range(4):
        pl.when(f == at)(functools.partial(add, mid01 if at < 2 else mid23, at % 2, at))


def last(me, mid01, mid23, early, late):
    _, patches, d = mid01.shape
    return pl.pallas_call(
        last_kernel,
        grid=(4,),
        in_specs=[SMEM] + [VMEM] * 10,
        out_specs=pl.BlockSpec((1, patches, d), lambda f: (f, 0, 0)),
        out_shape=jax.ShapeDtypeStruct((4, patches, d), BF16),
        compiler_params=pltpu.CompilerParams(vmem_limit_bytes=16 << 20),
        cost_estimate=pl.CostEstimate(
            flops=patches * d * 4, bytes_accessed=patches * d * 8, transcendentals=0
        ),
        name="last",
    )(me, mid01, mid23, *early, *late)


def exchange(pieces, masks):
    size = lax.axis_size("wide")
    return [pieces[0]] + [
        lax.ppermute(piece, "wide", [(w, w ^ mask) for w in range(size)])
        for piece, mask in zip(pieces[1:], masks[1:])
    ]


def shards(frames_in, qkv_spatial, out_spatial, qkv_temporal, out_temporal):
    me = lax.axis_index("wide").astype(jnp.int32).reshape(1)
    mid01, *pieces = spatial(me, frames_in, 0, 2, qkv_spatial, out_spatial, True, True)
    z_parts = exchange(regroup(exchange(pieces, OUTER)), INNER)
    mid23, *pieces = spatial(me, frames_in, 2, 2, qkv_spatial, out_spatial, False, False)
    y_parts = exchange(regroup(exchange(pieces, INNER)), OUTER)
    projected = project_early(z_parts, qkv_temporal)
    pieces = temporal(0, projected, y_parts, qkv_temporal, out_temporal, True)
    early = exchange(regroup(exchange(pieces, OUTER)), INNER)
    pieces = temporal(1, projected, y_parts, qkv_temporal, out_temporal, False)
    late = exchange(regroup(exchange(pieces, INNER)), OUTER)
    return last(me, mid01, mid23, early, late)


def solution(mesh):
    wide = mesh.shape["wide"]

    def whole(frames_in, *weights):
        local = frames_in.shape[0] // (wide * mesh.shape["groups"])
        fits = wide == 16 and local == 4 and frames_in.shape[1] == wide * TILE
        return jax.shard_map(
            shards if fits else plain_shards,
            mesh=mesh,
            in_specs=(P(("groups", "wide"), None, None), P(), P(), P(), P()),
            out_specs=P(("groups", "wide"), None, None),
            check_vma=False,
        )(frames_in, *weights)

    return whole
```

```python
import functools

import jax
import jax.numpy as jnp
from jax import lax
from jax.experimental import pallas as pl
from jax.experimental.pallas import tpu as pltpu
from jax.sharding import PartitionSpec as P

HEADS = 12
HEAD_DIM = 64
LANES = 128
TILE = 16
HALF = TILE // 2
GROUP = 256
LAG = 1
BF16 = jnp.bfloat16
F32 = jnp.float32
VMEM = pl.BlockSpec(memory_space=pltpu.VMEM)
SMEM = pl.BlockSpec(memory_space=pltpu.SMEM)
HBM = pl.BlockSpec(memory_space=pltpu.HBM)

OUTER = (0, 8, 12, 4)
INNER = (0, 1, 2, 3)


def normalize(floats):
    average = jnp.mean(floats, axis=-1, keepdims=True)
    centred = floats - average
    spread = jnp.mean(centred * centred, axis=-1, keepdims=True)
    return (centred * lax.rsqrt(spread + 1e-06)).astype(BF16)


def project(flat_rows, matrix):
    return jnp.dot(flat_rows, matrix, preferred_element_type=F32)


def plain_attend(projected, score_form, mix_form):
    leading = projected.shape[:-1]
    split = projected.reshape(leading + (3, HEADS, HEAD_DIM))
    queries = split[..., 0, :, :]
    key_part = split[..., 1, :, :]
    values = split[..., 2, :, :]
    scores = jnp.einsum(
        score_form, queries, key_part, preferred_element_type=F32
    ) * HEAD_DIM ** (-0.5)
    weights = jax.nn.softmax(scores, axis=-1).astype(BF16)
    mixed = jnp.einsum(mix_form, weights, values, preferred_element_type=F32)
    return mixed.reshape(leading + (HEADS * HEAD_DIM,)).astype(BF16)


def attend_time(received):
    frame_total, single, item_count, columns = received.shape
    sequences = received.reshape(frame_total, item_count, columns)
    result = plain_attend(sequences, "qbhd,kbhd->bhqk", "bhqk,kbhd->qbhd")
    return result.reshape(frame_total, single, item_count, HEADS * HEAD_DIM)


def plain_shards(frames_in, qkv_spatial, out_spatial, qkv_temporal, out_temporal):
    frame_count, patch_count, features = frames_in.shape
    wide_count = lax.axis_size("wide")
    per_group = patch_count // wide_count
    first = normalize(frames_in.astype(F32))
    proj_one = project(first.reshape(-1, features), qkv_spatial).astype(BF16)
    proj_one = proj_one.reshape(frame_count, patch_count, 3 * features)
    spatial = plain_attend(proj_one, "bqhd,bkhd->bhqk", "bhqk,bkhd->bqhd")
    update = project(spatial.reshape(-1, features), out_spatial).reshape(
        frame_count, patch_count, features
    )
    middle = (frames_in.astype(F32) + update).astype(BF16)
    second = normalize(middle.astype(F32))
    grouped = second.reshape(frame_count, wide_count, per_group, features)
    received = lax.all_to_all(grouped, "wide", split_axis=1, concat_axis=0, tiled=True)
    frame_total, single, item_count, columns = received.shape
    local_proj = project(received.reshape(-1, columns), qkv_temporal).astype(BF16)
    local_proj = local_proj.reshape(frame_total, single, item_count, 3 * columns)
    temporal = attend_time(local_proj)
    returned = lax.all_to_all(temporal, "wide", split_axis=0, concat_axis=1, tiled=True)
    change = project(returned.reshape(-1, features), out_temporal).reshape(
        frame_count, patch_count, features
    )
    return (middle.astype(F32) + change).astype(BF16)


def project_rows(a, wqkv, qkv, places, j):
    d = a.shape[1]
    for start in range(j * d, (j + 1) * d, GROUP):
        cols = slice(start, start + GROUP)
        part = jnp.dot(a[...], wqkv[:, cols], preferred_element_type=F32).astype(BF16)
        part = part * BF16(HEAD_DIM**-0.5) if j == 0 else part
        size = a.shape[0] // len(places)
        for n, place in enumerate(places):
            qkv[place : place + size, cols] = part[n * size : (n + 1) * size]


def attend(qkv, mixed, blocks, bias=None):
    d = mixed.shape[1]
    units = [(r, c, half) for r in blocks for c in range(0, d, LANES) for half in range(2)]
    size = blocks[0].stop - blocks[0].start
    low = lax.broadcasted_iota(jnp.int32, (size, LANES), 1) < HEAD_DIM
    begun, sums = {}, {}

    def begin(n):
        r, c, half = units[n]
        q = qkv[r, c : c + LANES]
        one = jnp.where(low if half == 0 else ~low, q, jnp.zeros_like(q))
        scores = lax.dot_general(
            one,
            qkv[r, d + c : d + c + LANES],
            (((1,), (1,)), ((), ())),
            preferred_element_type=F32,
        )
        if bias is not None:
            scores = scores + bias[...]
        begun[n] = scores, jnp.max(scores, axis=-1, keepdims=True)

    def end(n):
        r, c, half = units[n]
        scores, top = begun.pop(n)
        weights = jnp.exp(scores - top).astype(BF16)
        v = qkv[r, 2 * d + c : 2 * d + c + LANES]
        values = jnp.where(low if half == 0 else ~low, v, jnp.ones_like(v))
        sums[half] = jnp.dot(weights, values, preferred_element_type=F32)
        if half == 1:
            total = pltpu.roll(jnp.where(low, sums[1], sums[0]), HEAD_DIM, 1)
            mixed[r, c : c + LANES] = (jnp.where(low, sums[0], sums[1]) / total).astype(BF16)

    for n in range(len(units) + LAG):
        if n < len(units):
            begin(n)
        if n >= LAG:
            end(n - LAG)


def spatial_kernel(outer_first, begin, fetch, me, x_in, wqkv_in, wo_in, middle, *refs):
    frames, patches, d = middle.shape
    outs, (a, qkv, mixed, second, *held) = refs[:4], refs[4:]
    number = me[0]
    if fetch:
        x, wqkv, wo, sems = held
        pairs = [(x_in.at[pl.ds(begin, frames)], x)]
        pairs += [(wqkv_in.at[:, pl.ds(j * d, d)], wqkv.at[:, pl.ds(j * d, d)]) for j in range(3)]
        pairs += [(wo_in, wo)]
        copies = [pltpu.make_async_copy(*pair, sems.at[n]) for n, pair in enumerate(pairs)]
        for copy in copies:
            copy.start()
        copies[0].wait()
    else:
        x, wqkv, wo = x_in.at[pl.ds(begin, frames)], wqkv_in, wo_in
    for f in range(frames):
        a[f * patches : (f + 1) * patches, :] = normalize(x[f].astype(F32))
    for j in range(3):
        if fetch:
            copies[1 + j].wait()
        project_rows(a, wqkv, qkv, (0,), j)
    if fetch:
        copies[4].wait()
    attend(qkv, mixed, [slice(f * patches, (f + 1) * patches) for f in range(frames)])
    for f in range(frames):
        r = slice(f * patches, (f + 1) * patches)
        update = jnp.dot(mixed[r, :], wo[...], preferred_element_type=F32)
        mid = (x[f].astype(F32) + update).astype(BF16)
        middle[f] = mid
        second[...] = normalize(mid.astype(F32))
        for p in range(4):
            for i in range(4):
                owner = number ^ (OUTER[p] ^ INNER[i])
                rows = second[pl.ds(pl.multiple_of(owner * TILE, TILE), TILE), :]
                if outer_first:
                    outs[p][f, i] = rows
                else:
                    outs[i][f, p] = rows


def spatial(me, x, begin, frames, wqkv, wo, outer_first, fetch):
    _, patches, d = x.shape
    rows = frames * patches
    block = jax.ShapeDtypeStruct((frames, 4, TILE, d), BF16)
    held = [
        pltpu.VMEM((frames, patches, d), BF16),
        pltpu.VMEM(wqkv.shape, BF16),
        pltpu.VMEM(wo.shape, BF16),
        pltpu.SemaphoreType.DMA((5,)),
    ]
    return pl.pallas_call(
        functools.partial(spatial_kernel, outer_first, begin, fetch),
        in_specs=[SMEM] + [HBM if fetch else VMEM] * 3,
        out_specs=[VMEM] * 5,
        out_shape=[jax.ShapeDtypeStruct((frames, patches, d), BF16)] + [block] * 4,
        scratch_shapes=[
            pltpu.VMEM((rows, d), BF16),
            pltpu.VMEM((rows, 3 * d), BF16),
            pltpu.VMEM((rows, d), BF16),
            pltpu.VMEM((patches, d), BF16),
        ]
        + (held if fetch else []),
        compiler_params=pltpu.CompilerParams(vmem_limit_bytes=(52 if fetch else 24) << 20),
        cost_estimate=pl.CostEstimate(
            flops=8 * rows * d * d + 16 * rows * patches * d,
            bytes_accessed=8 * d * d,
            transcendentals=rows * patches * HEADS,
        ),
        name="spatial_outer" if outer_first else "spatial_inner",
    )(me, x, wqkv, wo)


def regroup_kernel(*refs):
    ins, outs = refs[:4], refs[4:]
    for b in range(4):
        for a in range(4):
            if len(ins[0].shape) == 4:
                outs[b][a] = ins[a][:, b]
            else:
                outs[b][a] = ins[a][b]


def regroup(pieces):
    shape = pieces[0].shape
    shape = (4, shape[0]) + shape[2:] if len(shape) == 4 else shape
    return pl.pallas_call(
        regroup_kernel,
        in_specs=[VMEM] * 4,
        out_specs=[VMEM] * 4,
        out_shape=[jax.ShapeDtypeStruct(shape, BF16)] * 4,
        compiler_params=pltpu.CompilerParams(vmem_limit_bytes=4 << 20),
        cost_estimate=pl.CostEstimate(flops=0, bytes_accessed=1 << 20, transcendentals=0),
        name="regroup",
    )(*pieces)


def halves_kernel(*refs):
    ins, outs = refs[:4], refs[4:]
    for i in range(4):
        for p in range(4):
            tiles = [ins[i][f, p].astype(F32) for f in range(2)]
            for half in range(2):
                rows = [tile[half * HALF : (half + 1) * HALF] for tile in tiles]
                outs[4 * half + p][i] = jnp.concatenate(rows, axis=0).astype(BF16)


def halves(pieces):
    shape = (4,) + pieces[0].shape[2:]
    blocks = pl.pallas_call(
        halves_kernel,
        in_specs=[VMEM] * 4,
        out_specs=[VMEM] * 8,
        out_shape=[jax.ShapeDtypeStruct(shape, BF16)] * 8,
        compiler_params=pltpu.CompilerParams(vmem_limit_bytes=4 << 20),
        cost_estimate=pl.CostEstimate(flops=0, bytes_accessed=1 << 20, transcendentals=0),
        name="halves",
    )(*pieces)
    return blocks[:4], blocks[4:]


def chosen(rows, columns, source):
    r = lax.broadcasted_iota(jnp.int32, (rows, columns), 0)
    c = lax.broadcasted_iota(jnp.int32, (rows, columns), 1)
    return (c == source(r)).astype(F32).astype(BF16)


def project_kernel(*refs):
    parts, wqkv, qkv, scratch, a = refs[:4], *refs[4:]
    length = 2 * TILE
    pick = chosen(TILE * TILE, TILE * TILE, lambda r: r % TILE * TILE + r // TILE)
    for block in range(2):
        for n in range(TILE):
            p, i, f = 2 * block + n // 8, n // 2 % 4, n % 2
            scratch[n * TILE : (n + 1) * TILE, :] = parts[i][p, f]
        taken = jnp.dot(pick, scratch[...], preferred_element_type=F32).astype(BF16)
        for q in range(TILE):
            start = q * length + block * TILE
            a[start : start + TILE, :] = taken[q * TILE : (q + 1) * TILE]
    for j in range(3):
        project_rows(a, wqkv, qkv, (0,), j)


def project_early(parts, wqkv):
    d = wqkv.shape[0]
    rows = TILE * 2 * TILE
    return pl.pallas_call(
        project_kernel,
        in_specs=[VMEM] * 5,
        out_specs=VMEM,
        out_shape=jax.ShapeDtypeStruct((rows, 3 * d), BF16),
        scratch_shapes=[pltpu.VMEM((TILE * TILE, d), BF16), pltpu.VMEM((rows, d), BF16)],
        compiler_params=pltpu.CompilerParams(vmem_limit_bytes=24 << 20),
        cost_estimate=pl.CostEstimate(
            flops=6 * rows * d * d, bytes_accessed=6 * d * d, transcendentals=0
        ),
        name="project_early",
    )(*parts, wqkv)


def temporal_kernel(half, outer_first, me, early, *refs):
    parts, wqkv, wo, outs = refs[:4], refs[4], refs[5], refs[6:10]
    scratch, a, qkv, mixed, change, bias = refs[10:]
    length = 2 * TILE
    run = 4 * length
    row, column = (lax.broadcasted_iota(jnp.int32, bias.shape, axis) for axis in range(2))
    other = ((row ^ column) & (run - length)) != 0
    bias[...] = jnp.where(other, -jnp.inf, 0.0)
    for p in range(4):
        for i in range(4):
            start = (4 * p + i) * TILE
            scratch[start : start + TILE, :] = parts[p][i]
    pick = chosen(
        HALF * length,
        HALF * length,
        lambda r: r % length // 2 * TILE + r % 2 * HALF + r // length,
    )
    a[...] = jnp.dot(pick, scratch[...], preferred_element_type=F32).astype(BF16)
    groups = range(HALF // 4)
    for g in groups:
        first = (half * HALF + 4 * g) * length
        qkv[2 * g * run : (2 * g + 1) * run, :] = early[first : first + run, :]
    for j in range(3):
        project_rows(a, wqkv, qkv, [(2 * g + 1) * run for g in groups], j)
    attend(qkv, mixed, [slice(2 * g * run, 2 * (g + 1) * run) for g in groups], bias)
    change[...] = jnp.dot(mixed[...], wo[...], preferred_element_type=F32).astype(BF16)
    back = chosen(HALF * TILE, HALF * TILE, lambda r: (r % HALF) * TILE + r // HALF)
    for chunk in range(2):
        for block in range(2):
            starts = [
                (q // 4 * 2 + chunk) * run + q % 4 * length + block * TILE for q in range(HALF)
            ]
            rows = jnp.concatenate([change[start : start + TILE, :] for start in starts], axis=0)
            rows = jnp.dot(back, rows, preferred_element_type=F32).astype(BF16)
            for n in range(8):
                p, i = 2 * block + n // 4, n % 4
                tile = rows[n * TILE : (n + 1) * TILE]
                at = slice(chunk * TILE, (chunk + 1) * TILE)
                if outer_first:
                    outs[p][i, at] = tile
                else:
                    outs[i][p, at] = tile


def temporal(me, half, early, parts, wqkv, wo, outer_first):
    d = wo.shape[0]
    rows = HALF * 2 * TILE
    block = jax.ShapeDtypeStruct((4, 2 * TILE, d), BF16)
    return pl.pallas_call(
        functools.partial(temporal_kernel, half, outer_first),
        in_specs=[SMEM] + [VMEM] * 7,
        out_specs=[VMEM] * 4,
        out_shape=[block] * 4,
        scratch_shapes=[
            pltpu.VMEM((TILE * TILE, d), BF16),
            pltpu.VMEM((rows, d), BF16),
            pltpu.VMEM((2 * rows, 3 * d), BF16),
            pltpu.VMEM((2 * rows, d), BF16),
            pltpu.VMEM((2 * rows, d), BF16),
            pltpu.VMEM((16 * TILE, 16 * TILE), F32),
        ],
        compiler_params=pltpu.CompilerParams(vmem_limit_bytes=24 << 20),
        cost_estimate=pl.CostEstimate(
            flops=10 * rows * d * d + 32 * rows * GROUP * d,
            bytes_accessed=8 * d * d,
            transcendentals=2 * rows * GROUP * HEADS,
        ),
        name="temporal",
    )(me, early, *parts, wqkv, wo)


def last_kernel(me, mid01, mid23, *refs):
    early, late, out = refs[:4], refs[4:8], refs[8]
    number = me[0]
    f = pl.program_id(0)

    def add(mid, frame, at):
        for p in range(4):
            for i in range(4):
                owner = number ^ (OUTER[p] ^ INNER[i])
                rows = pl.ds(pl.multiple_of(owner * TILE, TILE), TILE)
                change = jnp.concatenate(
                    [
                        early[i][p].astype(F32)[at * HALF : (at + 1) * HALF],
                        late[p][i].astype(F32)[at * HALF : (at + 1) * HALF],
                    ],
                    axis=0,
                )
                out[0, rows, :] = (mid[frame, rows, :].astype(F32) + change).astype(BF16)

    for at in range(4):
        pl.when(f == at)(functools.partial(add, mid01 if at < 2 else mid23, at % 2, at))


def last(me, mid01, mid23, early, late):
    _, patches, d = mid01.shape
    return pl.pallas_call(
        last_kernel,
        grid=(4,),
        in_specs=[SMEM] + [VMEM] * 10,
        out_specs=pl.BlockSpec((1, patches, d), lambda f: (f, 0, 0)),
        out_shape=jax.ShapeDtypeStruct((4, patches, d), BF16),
        compiler_params=pltpu.CompilerParams(vmem_limit_bytes=16 << 20),
        cost_estimate=pl.CostEstimate(
            flops=patches * d * 4, bytes_accessed=patches * d * 8, transcendentals=0
        ),
        name="last",
    )(me, mid01, mid23, *early, *late)


def after(block, earlier):
    return lax.optimization_barrier((block, earlier))[0]


def exchange(pieces, masks):
    size = lax.axis_size("wide")
    return [pieces[0]] + [
        lax.ppermute(piece, "wide", [(w, w ^ mask) for w in range(size)])
        for piece, mask in zip(pieces[1:], masks[1:])
    ]


def shards(frames_in, qkv_spatial, out_spatial, qkv_temporal, out_temporal):
    me = lax.axis_index("wide").astype(jnp.int32).reshape(1)
    mid01, *pieces = spatial(me, frames_in, 0, 2, qkv_spatial, out_spatial, True, True)
    z_parts = exchange(regroup(exchange(pieces, OUTER)), INNER)
    mid23, *pieces = spatial(me, frames_in, 2, 2, qkv_spatial, out_spatial, False, False)
    first_half, second_half = halves(exchange(pieces, INNER))
    first_half = exchange(first_half, OUTER)
    projected = project_early(z_parts, qkv_temporal)
    pieces = temporal(me, 0, projected, first_half, qkv_temporal, out_temporal, True)
    early = exchange(regroup(exchange(pieces, OUTER)), INNER)
    second_half = after(second_half, projected)
    second_half = exchange(second_half, OUTER)
    pieces = temporal(me, 1, projected, second_half, qkv_temporal, out_temporal, False)
    late = exchange(regroup(exchange(pieces, INNER)), OUTER)
    return last(me, mid01, mid23, early, late)


def solution(mesh):
    wide = mesh.shape["wide"]

    def whole(frames_in, *weights):
        local = frames_in.shape[0] // (wide * mesh.shape["groups"])
        fits = wide == 16 and local == 4 and frames_in.shape[1] == wide * TILE
        return jax.shard_map(
            shards if fits else plain_shards,
            mesh=mesh,
            in_specs=(P(("groups", "wide"), None, None), P(), P(), P(), P()),
            out_specs=P(("groups", "wide"), None, None),
            check_vma=False,
        )(frames_in, *weights)

    return whole
```

```python
import functools

import jax
import jax.numpy as jnp
from jax import lax
from jax.experimental import pallas as pl
from jax.experimental.pallas import tpu as pltpu
from jax.sharding import PartitionSpec as P

HEADS = 12
HEAD_DIM = 64
LANES = 128
TILE = 16
HALF = TILE // 2
GROUP = 256
LAG = 1
BF16 = jnp.bfloat16
F32 = jnp.float32
VMEM = pl.BlockSpec(memory_space=pltpu.VMEM)
SMEM = pl.BlockSpec(memory_space=pltpu.SMEM)
HBM = pl.BlockSpec(memory_space=pltpu.HBM)

OUTER = (0, 8, 12, 4)
INNER = (0, 2, 3, 1)


def normalize(floats):
    average = jnp.mean(floats, axis=-1, keepdims=True)
    centred = floats - average
    spread = jnp.mean(centred * centred, axis=-1, keepdims=True)
    return (centred * lax.rsqrt(spread + 1e-06)).astype(BF16)


def project(flat_rows, matrix):
    return jnp.dot(flat_rows, matrix, preferred_element_type=F32)


def plain_attend(projected, score_form, mix_form):
    leading = projected.shape[:-1]
    split = projected.reshape(leading + (3, HEADS, HEAD_DIM))
    queries = split[..., 0, :, :]
    key_part = split[..., 1, :, :]
    values = split[..., 2, :, :]
    scores = jnp.einsum(
        score_form, queries, key_part, preferred_element_type=F32
    ) * HEAD_DIM ** (-0.5)
    weights = jax.nn.softmax(scores, axis=-1).astype(BF16)
    mixed = jnp.einsum(mix_form, weights, values, preferred_element_type=F32)
    return mixed.reshape(leading + (HEADS * HEAD_DIM,)).astype(BF16)


def attend_time(received):
    frame_total, single, item_count, columns = received.shape
    sequences = received.reshape(frame_total, item_count, columns)
    result = plain_attend(sequences, "qbhd,kbhd->bhqk", "bhqk,kbhd->qbhd")
    return result.reshape(frame_total, single, item_count, HEADS * HEAD_DIM)


def plain_shards(frames_in, qkv_spatial, out_spatial, qkv_temporal, out_temporal):
    frame_count, patch_count, features = frames_in.shape
    wide_count = lax.axis_size("wide")
    per_group = patch_count // wide_count
    first = normalize(frames_in.astype(F32))
    proj_one = project(first.reshape(-1, features), qkv_spatial).astype(BF16)
    proj_one = proj_one.reshape(frame_count, patch_count, 3 * features)
    spatial = plain_attend(proj_one, "bqhd,bkhd->bhqk", "bhqk,bkhd->bqhd")
    update = project(spatial.reshape(-1, features), out_spatial).reshape(
        frame_count, patch_count, features
    )
    middle = (frames_in.astype(F32) + update).astype(BF16)
    second = normalize(middle.astype(F32))
    grouped = second.reshape(frame_count, wide_count, per_group, features)
    received = lax.all_to_all(grouped, "wide", split_axis=1, concat_axis=0, tiled=True)
    frame_total, single, item_count, columns = received.shape
    local_proj = project(received.reshape(-1, columns), qkv_temporal).astype(BF16)
    local_proj = local_proj.reshape(frame_total, single, item_count, 3 * columns)
    temporal = attend_time(local_proj)
    returned = lax.all_to_all(temporal, "wide", split_axis=0, concat_axis=1, tiled=True)
    change = project(returned.reshape(-1, features), out_temporal).reshape(
        frame_count, patch_count, features
    )
    return (middle.astype(F32) + change).astype(BF16)


def project_rows(a, wqkv, qkv, places, j):
    d = a.shape[1]
    for start in range(j * d, (j + 1) * d, GROUP):
        cols = slice(start, start + GROUP)
        part = jnp.dot(a[...], wqkv[:, cols], preferred_element_type=F32).astype(BF16)
        part = part * BF16(HEAD_DIM**-0.5) if j == 0 else part
        size = a.shape[0] // len(places)
        for n, place in enumerate(places):
            qkv[place : place + size, cols] = part[n * size : (n + 1) * size]


def attend(qkv, mixed, blocks, bias=None):
    d = mixed.shape[1]
    units = [(r, c, half) for r in blocks for c in range(0, d, LANES) for half in range(2)]
    size = blocks[0].stop - blocks[0].start
    low = lax.broadcasted_iota(jnp.int32, (size, LANES), 1) < HEAD_DIM
    begun, sums = {}, {}

    def begin(n):
        r, c, half = units[n]
        q = qkv[r, c : c + LANES]
        one = jnp.where(low if half == 0 else ~low, q, jnp.zeros_like(q))
        scores = lax.dot_general(
            one,
            qkv[r, d + c : d + c + LANES],
            (((1,), (1,)), ((), ())),
            preferred_element_type=F32,
        )
        if bias is not None:
            scores = scores + bias[...]
        begun[n] = scores, jnp.max(scores, axis=-1, keepdims=True)

    def end(n):
        r, c, half = units[n]
        scores, top = begun.pop(n)
        weights = jnp.exp(scores - top).astype(BF16)
        v = qkv[r, 2 * d + c : 2 * d + c + LANES]
        values = jnp.where(low if half == 0 else ~low, v, jnp.ones_like(v))
        sums[half] = jnp.dot(weights, values, preferred_element_type=F32)
        if half == 1:
            total = pltpu.roll(jnp.where(low, sums[1], sums[0]), HEAD_DIM, 1)
            mixed[r, c : c + LANES] = (jnp.where(low, sums[0], sums[1]) / total).astype(BF16)

    for n in range(len(units) + LAG):
        if n < len(units):
            begin(n)
        if n >= LAG:
            end(n - LAG)


def spatial_kernel(outer_first, begin, fetch, me, x_in, wqkv_in, wo_in, middle, *refs):
    frames, patches, d = middle.shape
    outs, (a, qkv, mixed, second, *held) = refs[:4], refs[4:]
    number = me[0]
    if fetch:
        x, wqkv, wo, sems = held
        pairs = [(x_in.at[pl.ds(begin, frames)], x)]
        pairs += [(wqkv_in.at[:, pl.ds(j * d, d)], wqkv.at[:, pl.ds(j * d, d)]) for j in range(3)]
        pairs += [(wo_in, wo)]
        copies = [pltpu.make_async_copy(*pair, sems.at[n]) for n, pair in enumerate(pairs)]
        for copy in copies:
            copy.start()
        copies[0].wait()
    else:
        x, wqkv, wo = x_in.at[pl.ds(begin, frames)], wqkv_in, wo_in
    for f in range(frames):
        a[f * patches : (f + 1) * patches, :] = normalize(x[f].astype(F32))
    for j in range(3):
        if fetch:
            copies[1 + j].wait()
        project_rows(a, wqkv, qkv, (0,), j)
    if fetch:
        copies[4].wait()
    attend(qkv, mixed, [slice(f * patches, (f + 1) * patches) for f in range(frames)])
    for f in range(frames):
        r = slice(f * patches, (f + 1) * patches)
        update = jnp.dot(mixed[r, :], wo[...], preferred_element_type=F32)
        mid = (x[f].astype(F32) + update).astype(BF16)
        middle[f] = mid
        second[...] = normalize(mid.astype(F32))
        for p in range(4):
            for i in range(4):
                owner = number ^ (OUTER[p] ^ INNER[i])
                rows = second[pl.ds(pl.multiple_of(owner * TILE, TILE), TILE), :]
                if outer_first:
                    outs[p][f, i] = rows
                else:
                    outs[i][f, p] = rows


def spatial(me, x, begin, frames, wqkv, wo, outer_first, fetch):
    _, patches, d = x.shape
    rows = frames * patches
    block = jax.ShapeDtypeStruct((frames, 4, TILE, d), BF16)
    held = [
        pltpu.VMEM((frames, patches, d), BF16),
        pltpu.VMEM(wqkv.shape, BF16),
        pltpu.VMEM(wo.shape, BF16),
        pltpu.SemaphoreType.DMA((5,)),
    ]
    return pl.pallas_call(
        functools.partial(spatial_kernel, outer_first, begin, fetch),
        in_specs=[SMEM] + [HBM if fetch else VMEM] * 3,
        out_specs=[VMEM] * 5,
        out_shape=[jax.ShapeDtypeStruct((frames, patches, d), BF16)] + [block] * 4,
        scratch_shapes=[
            pltpu.VMEM((rows, d), BF16),
            pltpu.VMEM((rows, 3 * d), BF16),
            pltpu.VMEM((rows, d), BF16),
            pltpu.VMEM((patches, d), BF16),
        ]
        + (held if fetch else []),
        compiler_params=pltpu.CompilerParams(vmem_limit_bytes=(52 if fetch else 24) << 20),
        cost_estimate=pl.CostEstimate(
            flops=8 * rows * d * d + 16 * rows * patches * d,
            bytes_accessed=8 * d * d,
            transcendentals=rows * patches * HEADS,
        ),
        name="spatial_outer" if outer_first else "spatial_inner",
    )(me, x, wqkv, wo)


def regroup_kernel(*refs):
    ins, outs = refs[:4], refs[4:]
    for b in range(4):
        for a in range(4):
            if len(ins[0].shape) == 4:
                outs[b][a] = ins[a][:, b]
            else:
                outs[b][a] = ins[a][b]


def regroup(pieces):
    shape = pieces[0].shape
    shape = (4, shape[0]) + shape[2:] if len(shape) == 4 else shape
    return pl.pallas_call(
        regroup_kernel,
        in_specs=[VMEM] * 4,
        out_specs=[VMEM] * 4,
        out_shape=[jax.ShapeDtypeStruct(shape, BF16)] * 4,
        compiler_params=pltpu.CompilerParams(vmem_limit_bytes=4 << 20),
        cost_estimate=pl.CostEstimate(flops=0, bytes_accessed=1 << 20, transcendentals=0),
        name="regroup",
    )(*pieces)


def halves_kernel(*refs):
    ins, outs = refs[:4], refs[4:]
    for i in range(4):
        for p in range(4):
            tiles = [ins[i][f, p].astype(F32) for f in range(2)]
            for half in range(2):
                rows = [tile[half * HALF : (half + 1) * HALF] for tile in tiles]
                outs[4 * half + p][i] = jnp.concatenate(rows, axis=0).astype(BF16)


def halves(pieces):
    shape = (4,) + pieces[0].shape[2:]
    blocks = pl.pallas_call(
        halves_kernel,
        in_specs=[VMEM] * 4,
        out_specs=[VMEM] * 8,
        out_shape=[jax.ShapeDtypeStruct(shape, BF16)] * 8,
        compiler_params=pltpu.CompilerParams(vmem_limit_bytes=4 << 20),
        cost_estimate=pl.CostEstimate(flops=0, bytes_accessed=1 << 20, transcendentals=0),
        name="halves",
    )(*pieces)
    return blocks[:4], blocks[4:]


def chosen(rows, columns, source):
    r = lax.broadcasted_iota(jnp.int32, (rows, columns), 0)
    c = lax.broadcasted_iota(jnp.int32, (rows, columns), 1)
    return (c == source(r)).astype(F32).astype(BF16)


def project_kernel(*refs):
    parts, wqkv, qkv, scratch, a = refs[:4], *refs[4:]
    length = 2 * TILE
    pick = chosen(TILE * TILE, TILE * TILE, lambda r: r % TILE * TILE + r // TILE)
    for block in range(2):
        for n in range(TILE):
            p, i, f = 2 * block + n // 8, n // 2 % 4, n % 2
            scratch[n * TILE : (n + 1) * TILE, :] = parts[i][p, f]
        taken = jnp.dot(pick, scratch[...], preferred_element_type=F32).astype(BF16)
        for q in range(TILE):
            start = q * length + block * TILE
            a[start : start + TILE, :] = taken[q * TILE : (q + 1) * TILE]
    for j in range(3):
        project_rows(a, wqkv, qkv, (0,), j)


def project_early(parts, wqkv):
    d = wqkv.shape[0]
    rows = TILE * 2 * TILE
    return pl.pallas_call(
        project_kernel,
        in_specs=[VMEM] * 5,
        out_specs=VMEM,
        out_shape=jax.ShapeDtypeStruct((rows, 3 * d), BF16),
        scratch_shapes=[pltpu.VMEM((TILE * TILE, d), BF16), pltpu.VMEM((rows, d), BF16)],
        compiler_params=pltpu.CompilerParams(vmem_limit_bytes=24 << 20),
        cost_estimate=pl.CostEstimate(
            flops=6 * rows * d * d, bytes_accessed=6 * d * d, transcendentals=0
        ),
        name="project_early",
    )(*parts, wqkv)


def temporal_kernel(half, outer_first, me, early, *refs):
    parts, wqkv, wo, outs = refs[:4], refs[4], refs[5], refs[6:10]
    scratch, a, qkv, mixed, change, bias = refs[10:]
    length = 2 * TILE
    run = 4 * length
    row, column = (lax.broadcasted_iota(jnp.int32, bias.shape, axis) for axis in range(2))
    other = ((row ^ column) & (run - length)) != 0
    bias[...] = jnp.where(other, -jnp.inf, 0.0)
    for p in range(4):
        for i in range(4):
            start = (4 * p + i) * TILE
            scratch[start : start + TILE, :] = parts[p][i]
    pick = chosen(
        HALF * length,
        HALF * length,
        lambda r: r % length // 2 * TILE + r % 2 * HALF + r // length,
    )
    a[...] = jnp.dot(pick, scratch[...], preferred_element_type=F32).astype(BF16)
    groups = range(HALF // 4)
    for g in groups:
        first = (half * HALF + 4 * g) * length
        qkv[2 * g * run : (2 * g + 1) * run, :] = early[first : first + run, :]
    for j in range(3):
        project_rows(a, wqkv, qkv, [(2 * g + 1) * run for g in groups], j)
    attend(qkv, mixed, [slice(2 * g * run, 2 * (g + 1) * run) for g in groups], bias)
    change[...] = jnp.dot(mixed[...], wo[...], preferred_element_type=F32).astype(BF16)
    back = chosen(HALF * TILE, HALF * TILE, lambda r: (r % HALF) * TILE + r // HALF)
    for chunk in range(2):
        for block in range(2):
            starts = [
                (q // 4 * 2 + chunk) * run + q % 4 * length + block * TILE for q in range(HALF)
            ]
            rows = jnp.concatenate([change[start : start + TILE, :] for start in starts], axis=0)
            rows = jnp.dot(back, rows, preferred_element_type=F32).astype(BF16)
            for n in range(8):
                p, i = 2 * block + n // 4, n % 4
                tile = rows[n * TILE : (n + 1) * TILE]
                at = slice(chunk * TILE, (chunk + 1) * TILE)
                if outer_first:
                    outs[p][i, at] = tile
                else:
                    outs[i][p, at] = tile


def temporal(me, half, early, parts, wqkv, wo, outer_first):
    d = wo.shape[0]
    rows = HALF * 2 * TILE
    block = jax.ShapeDtypeStruct((4, 2 * TILE, d), BF16)
    return pl.pallas_call(
        functools.partial(temporal_kernel, half, outer_first),
        in_specs=[SMEM] + [VMEM] * 7,
        out_specs=[VMEM] * 4,
        out_shape=[block] * 4,
        scratch_shapes=[
            pltpu.VMEM((TILE * TILE, d), BF16),
            pltpu.VMEM((rows, d), BF16),
            pltpu.VMEM((2 * rows, 3 * d), BF16),
            pltpu.VMEM((2 * rows, d), BF16),
            pltpu.VMEM((2 * rows, d), BF16),
            pltpu.VMEM((16 * TILE, 16 * TILE), F32),
        ],
        compiler_params=pltpu.CompilerParams(vmem_limit_bytes=24 << 20),
        cost_estimate=pl.CostEstimate(
            flops=10 * rows * d * d + 32 * rows * GROUP * d,
            bytes_accessed=8 * d * d,
            transcendentals=2 * rows * GROUP * HEADS,
        ),
        name="temporal",
    )(me, early, *parts, wqkv, wo)


def last_kernel(me, mid01, mid23, *refs):
    early, late, out = refs[:4], refs[4:8], refs[8]
    number = me[0]
    f = pl.program_id(0)

    def add(mid, frame, at):
        for p in range(4):
            for i in range(4):
                owner = number ^ (OUTER[p] ^ INNER[i])
                rows = pl.ds(pl.multiple_of(owner * TILE, TILE), TILE)
                change = jnp.concatenate(
                    [
                        early[i][p].astype(F32)[at * HALF : (at + 1) * HALF],
                        late[p][i].astype(F32)[at * HALF : (at + 1) * HALF],
                    ],
                    axis=0,
                )
                out[0, rows, :] = (mid[frame, rows, :].astype(F32) + change).astype(BF16)

    for at in range(4):
        pl.when(f == at)(functools.partial(add, mid01 if at < 2 else mid23, at % 2, at))


def last(me, mid01, mid23, early, late):
    _, patches, d = mid01.shape
    return pl.pallas_call(
        last_kernel,
        grid=(4,),
        in_specs=[SMEM] + [VMEM] * 10,
        out_specs=pl.BlockSpec((1, patches, d), lambda f: (f, 0, 0)),
        out_shape=jax.ShapeDtypeStruct((4, patches, d), BF16),
        compiler_params=pltpu.CompilerParams(vmem_limit_bytes=16 << 20),
        cost_estimate=pl.CostEstimate(
            flops=patches * d * 4, bytes_accessed=patches * d * 8, transcendentals=0
        ),
        name="last",
    )(me, mid01, mid23, *early, *late)


def after(block, earlier):
    return lax.optimization_barrier((block, earlier))[0]


def exchange(pieces, masks):
    size = lax.axis_size("wide")
    return [pieces[0]] + [
        lax.ppermute(piece, "wide", [(w, w ^ mask) for w in range(size)])
        for piece, mask in zip(pieces[1:], masks[1:])
    ]


def shards(frames_in, qkv_spatial, out_spatial, qkv_temporal, out_temporal):
    me = lax.axis_index("wide").astype(jnp.int32).reshape(1)
    mid01, *pieces = spatial(me, frames_in, 0, 2, qkv_spatial, out_spatial, True, True)
    z_parts = exchange(regroup(exchange(pieces, OUTER)), INNER)
    mid23, *pieces = spatial(me, frames_in, 2, 2, qkv_spatial, out_spatial, False, False)
    first_half, second_half = halves(exchange(pieces, INNER))
    first_half = exchange(first_half, OUTER)
    projected = project_early(z_parts, qkv_temporal)
    pieces = temporal(me, 0, projected, first_half, qkv_temporal, out_temporal, True)
    early = exchange(regroup(exchange(pieces, OUTER)), INNER)
    second_half = after(second_half, projected)
    second_half = exchange(second_half, OUTER)
    pieces = temporal(me, 1, projected, second_half, qkv_temporal, out_temporal, False)
    late = exchange(regroup(exchange(pieces, INNER)), OUTER)
    return last(me, mid01, mid23, early, late)


def solution(mesh):
    wide = mesh.shape["wide"]

    def whole(frames_in, *weights):
        local = frames_in.shape[0] // (wide * mesh.shape["groups"])
        fits = wide == 16 and local == 4 and frames_in.shape[1] == wide * TILE
        return jax.shard_map(
            shards if fits else plain_shards,
            mesh=mesh,
            in_specs=(P(("groups", "wide"), None, None), P(), P(), P(), P()),
            out_specs=P(("groups", "wide"), None, None),
            check_vma=False,
        )(frames_in, *weights)

    return whole
```

```python
import functools

import jax
import jax.numpy as jnp
from jax import lax
from jax.experimental import pallas as pl
from jax.experimental.pallas import tpu as pltpu
from jax.sharding import PartitionSpec as P

HEADS = 12
HEAD_DIM = 64
LANES = 128
TILE = 16
HALF = TILE // 2
GROUP = 256
LAG = 1
BF16 = jnp.bfloat16
F32 = jnp.float32
VMEM = pl.BlockSpec(memory_space=pltpu.VMEM)
SMEM = pl.BlockSpec(memory_space=pltpu.SMEM)
HBM = pl.BlockSpec(memory_space=pltpu.HBM)

OUTER = (0, 12, 8, 4)
INNER = (0, 2, 3, 1)


def normalize(floats):
    average = jnp.mean(floats, axis=-1, keepdims=True)
    centred = floats - average
    spread = jnp.mean(centred * centred, axis=-1, keepdims=True)
    return (centred * lax.rsqrt(spread + 1e-06)).astype(BF16)


def project(flat_rows, matrix):
    return jnp.dot(flat_rows, matrix, preferred_element_type=F32)


def plain_attend(projected, score_form, mix_form):
    leading = projected.shape[:-1]
    split = projected.reshape(leading + (3, HEADS, HEAD_DIM))
    queries = split[..., 0, :, :]
    key_part = split[..., 1, :, :]
    values = split[..., 2, :, :]
    scores = jnp.einsum(
        score_form, queries, key_part, preferred_element_type=F32
    ) * HEAD_DIM ** (-0.5)
    weights = jax.nn.softmax(scores, axis=-1).astype(BF16)
    mixed = jnp.einsum(mix_form, weights, values, preferred_element_type=F32)
    return mixed.reshape(leading + (HEADS * HEAD_DIM,)).astype(BF16)


def attend_time(received):
    frame_total, single, item_count, columns = received.shape
    sequences = received.reshape(frame_total, item_count, columns)
    result = plain_attend(sequences, "qbhd,kbhd->bhqk", "bhqk,kbhd->qbhd")
    return result.reshape(frame_total, single, item_count, HEADS * HEAD_DIM)


def plain_shards(frames_in, qkv_spatial, out_spatial, qkv_temporal, out_temporal):
    frame_count, patch_count, features = frames_in.shape
    wide_count = lax.axis_size("wide")
    per_group = patch_count // wide_count
    first = normalize(frames_in.astype(F32))
    proj_one = project(first.reshape(-1, features), qkv_spatial).astype(BF16)
    proj_one = proj_one.reshape(frame_count, patch_count, 3 * features)
    spatial = plain_attend(proj_one, "bqhd,bkhd->bhqk", "bhqk,bkhd->bqhd")
    update = project(spatial.reshape(-1, features), out_spatial).reshape(
        frame_count, patch_count, features
    )
    middle = (frames_in.astype(F32) + update).astype(BF16)
    second = normalize(middle.astype(F32))
    grouped = second.reshape(frame_count, wide_count, per_group, features)
    received = lax.all_to_all(grouped, "wide", split_axis=1, concat_axis=0, tiled=True)
    frame_total, single, item_count, columns = received.shape
    local_proj = project(received.reshape(-1, columns), qkv_temporal).astype(BF16)
    local_proj = local_proj.reshape(frame_total, single, item_count, 3 * columns)
    temporal = attend_time(local_proj)
    returned = lax.all_to_all(temporal, "wide", split_axis=0, concat_axis=1, tiled=True)
    change = project(returned.reshape(-1, features), out_temporal).reshape(
        frame_count, patch_count, features
    )
    return (middle.astype(F32) + change).astype(BF16)


def project_rows(a, wqkv, qkv, places, j):
    d = a.shape[1]
    for start in range(j * d, (j + 1) * d, GROUP):
        cols = slice(start, start + GROUP)
        part = jnp.dot(a[...], wqkv[:, cols], preferred_element_type=F32).astype(BF16)
        part = part * BF16(HEAD_DIM**-0.5) if j == 0 else part
        size = a.shape[0] // len(places)
        for n, place in enumerate(places):
            qkv[place : place + size, cols] = part[n * size : (n + 1) * size]


def attend(qkv, mixed, blocks, bias=None):
    d = mixed.shape[1]
    units = [(r, c, half) for r in blocks for c in range(0, d, LANES) for half in range(2)]
    size = blocks[0].stop - blocks[0].start
    low = lax.broadcasted_iota(jnp.int32, (size, LANES), 1) < HEAD_DIM
    begun, sums = {}, {}

    def begin(n):
        r, c, half = units[n]
        q = qkv[r, c : c + LANES]
        one = jnp.where(low if half == 0 else ~low, q, jnp.zeros_like(q))
        scores = lax.dot_general(
            one,
            qkv[r, d + c : d + c + LANES],
            (((1,), (1,)), ((), ())),
            preferred_element_type=F32,
        )
        if bias is not None:
            scores = scores + bias[...]
        begun[n] = scores, jnp.max(scores, axis=-1, keepdims=True)

    def end(n):
        r, c, half = units[n]
        scores, top = begun.pop(n)
        weights = jnp.exp(scores - top).astype(BF16)
        v = qkv[r, 2 * d + c : 2 * d + c + LANES]
        values = jnp.where(low if half == 0 else ~low, v, jnp.ones_like(v))
        sums[half] = jnp.dot(weights, values, preferred_element_type=F32)
        if half == 1:
            total = pltpu.roll(jnp.where(low, sums[1], sums[0]), HEAD_DIM, 1)
            mixed[r, c : c + LANES] = (jnp.where(low, sums[0], sums[1]) / total).astype(BF16)

    for n in range(len(units) + LAG):
        if n < len(units):
            begin(n)
        if n >= LAG:
            end(n - LAG)


def spatial_kernel(outer_first, begin, fetch, me, x_in, wqkv_in, wo_in, middle, *refs):
    frames, patches, d = middle.shape
    outs, (a, qkv, mixed, second, *held) = refs[:4], refs[4:]
    number = me[0]
    if fetch:
        x, wqkv, wo, sems = held
        pairs = [(x_in.at[pl.ds(begin, frames)], x)]
        pairs += [(wqkv_in.at[:, pl.ds(j * d, d)], wqkv.at[:, pl.ds(j * d, d)]) for j in range(3)]
        pairs += [(wo_in, wo)]
        copies = [pltpu.make_async_copy(*pair, sems.at[n]) for n, pair in enumerate(pairs)]
        for copy in copies:
            copy.start()
        copies[0].wait()
    else:
        x, wqkv, wo = x_in.at[pl.ds(begin, frames)], wqkv_in, wo_in
    for f in range(frames):
        a[f * patches : (f + 1) * patches, :] = normalize(x[f].astype(F32))
    for j in range(3):
        if fetch:
            copies[1 + j].wait()
        project_rows(a, wqkv, qkv, (0,), j)
    if fetch:
        copies[4].wait()
    attend(qkv, mixed, [slice(f * patches, (f + 1) * patches) for f in range(frames)])
    for f in range(frames):
        r = slice(f * patches, (f + 1) * patches)
        update = jnp.dot(mixed[r, :], wo[...], preferred_element_type=F32)
        mid = (x[f].astype(F32) + update).astype(BF16)
        middle[f] = mid
        second[...] = normalize(mid.astype(F32))
        for p in range(4):
            for i in range(4):
                owner = number ^ (OUTER[p] ^ INNER[i])
                rows = second[pl.ds(pl.multiple_of(owner * TILE, TILE), TILE), :]
                if outer_first:
                    outs[p][f, i] = rows
                else:
                    outs[i][f, p] = rows


def spatial(me, x, begin, frames, wqkv, wo, outer_first, fetch):
    _, patches, d = x.shape
    rows = frames * patches
    block = jax.ShapeDtypeStruct((frames, 4, TILE, d), BF16)
    held = [
        pltpu.VMEM((frames, patches, d), BF16),
        pltpu.VMEM(wqkv.shape, BF16),
        pltpu.VMEM(wo.shape, BF16),
        pltpu.SemaphoreType.DMA((5,)),
    ]
    return pl.pallas_call(
        functools.partial(spatial_kernel, outer_first, begin, fetch),
        in_specs=[SMEM] + [HBM if fetch else VMEM] * 3,
        out_specs=[VMEM] * 5,
        out_shape=[jax.ShapeDtypeStruct((frames, patches, d), BF16)] + [block] * 4,
        scratch_shapes=[
            pltpu.VMEM((rows, d), BF16),
            pltpu.VMEM((rows, 3 * d), BF16),
            pltpu.VMEM((rows, d), BF16),
            pltpu.VMEM((patches, d), BF16),
        ]
        + (held if fetch else []),
        compiler_params=pltpu.CompilerParams(vmem_limit_bytes=(52 if fetch else 24) << 20),
        cost_estimate=pl.CostEstimate(
            flops=8 * rows * d * d + 16 * rows * patches * d,
            bytes_accessed=8 * d * d,
            transcendentals=rows * patches * HEADS,
        ),
        name="spatial_outer" if outer_first else "spatial_inner",
    )(me, x, wqkv, wo)


def regroup_kernel(*refs):
    ins, outs = refs[:4], refs[4:]
    for b in range(4):
        for a in range(4):
            if len(ins[0].shape) == 4:
                outs[b][a] = ins[a][:, b]
            else:
                outs[b][a] = ins[a][b]


def regroup(pieces):
    shape = pieces[0].shape
    shape = (4, shape[0]) + shape[2:] if len(shape) == 4 else shape
    return pl.pallas_call(
        regroup_kernel,
        in_specs=[VMEM] * 4,
        out_specs=[VMEM] * 4,
        out_shape=[jax.ShapeDtypeStruct(shape, BF16)] * 4,
        compiler_params=pltpu.CompilerParams(vmem_limit_bytes=4 << 20),
        cost_estimate=pl.CostEstimate(flops=0, bytes_accessed=1 << 20, transcendentals=0),
        name="regroup",
    )(*pieces)


def halves_kernel(*refs):
    ins, outs = refs[:4], refs[4:]
    for i in range(4):
        for p in range(4):
            tiles = [ins[i][f, p].astype(F32) for f in range(2)]
            for half in range(2):
                rows = [tile[half * HALF : (half + 1) * HALF] for tile in tiles]
                outs[4 * half + p][i] = jnp.concatenate(rows, axis=0).astype(BF16)


def halves(pieces):
    shape = (4,) + pieces[0].shape[2:]
    blocks = pl.pallas_call(
        halves_kernel,
        in_specs=[VMEM] * 4,
        out_specs=[VMEM] * 8,
        out_shape=[jax.ShapeDtypeStruct(shape, BF16)] * 8,
        compiler_params=pltpu.CompilerParams(vmem_limit_bytes=4 << 20),
        cost_estimate=pl.CostEstimate(flops=0, bytes_accessed=1 << 20, transcendentals=0),
        name="halves",
    )(*pieces)
    return blocks[:4], blocks[4:]


def chosen(rows, columns, source):
    r = lax.broadcasted_iota(jnp.int32, (rows, columns), 0)
    c = lax.broadcasted_iota(jnp.int32, (rows, columns), 1)
    return (c == source(r)).astype(F32).astype(BF16)


def project_kernel(*refs):
    parts, wqkv, qkv, scratch, a = refs[:4], *refs[4:]
    length = 2 * TILE
    pick = chosen(TILE * TILE, TILE * TILE, lambda r: r % TILE * TILE + r // TILE)
    for block in range(2):
        for n in range(TILE):
            p, i, f = 2 * block + n // 8, n // 2 % 4, n % 2
            scratch[n * TILE : (n + 1) * TILE, :] = parts[i][p, f]
        taken = jnp.dot(pick, scratch[...], preferred_element_type=F32).astype(BF16)
        for q in range(TILE):
            start = q * length + block * TILE
            a[start : start + TILE, :] = taken[q * TILE : (q + 1) * TILE]
    for j in range(3):
        project_rows(a, wqkv, qkv, (0,), j)


def project_early(parts, wqkv):
    d = wqkv.shape[0]
    rows = TILE * 2 * TILE
    return pl.pallas_call(
        project_kernel,
        in_specs=[VMEM] * 5,
        out_specs=VMEM,
        out_shape=jax.ShapeDtypeStruct((rows, 3 * d), BF16),
        scratch_shapes=[pltpu.VMEM((TILE * TILE, d), BF16), pltpu.VMEM((rows, d), BF16)],
        compiler_params=pltpu.CompilerParams(vmem_limit_bytes=24 << 20),
        cost_estimate=pl.CostEstimate(
            flops=6 * rows * d * d, bytes_accessed=6 * d * d, transcendentals=0
        ),
        name="project_early",
    )(*parts, wqkv)


def temporal_kernel(half, outer_first, me, early, *refs):
    parts, wqkv, wo, outs = refs[:4], refs[4], refs[5], refs[6:10]
    scratch, a, qkv, mixed, change, bias = refs[10:]
    length = 2 * TILE
    run = 4 * length
    row, column = (lax.broadcasted_iota(jnp.int32, bias.shape, axis) for axis in range(2))
    other = ((row ^ column) & (run - length)) != 0
    bias[...] = jnp.where(other, -jnp.inf, 0.0)
    for p in range(4):
        for i in range(4):
            start = (4 * p + i) * TILE
            scratch[start : start + TILE, :] = parts[p][i]
    pick = chosen(
        HALF * length,
        HALF * length,
        lambda r: r % length // 2 * TILE + r % 2 * HALF + r // length,
    )
    a[...] = jnp.dot(pick, scratch[...], preferred_element_type=F32).astype(BF16)
    groups = range(HALF // 4)
    for g in groups:
        first = (half * HALF + 4 * g) * length
        qkv[2 * g * run : (2 * g + 1) * run, :] = early[first : first + run, :]
    for j in range(3):
        project_rows(a, wqkv, qkv, [(2 * g + 1) * run for g in groups], j)
    attend(qkv, mixed, [slice(2 * g * run, 2 * (g + 1) * run) for g in groups], bias)
    change[...] = jnp.dot(mixed[...], wo[...], preferred_element_type=F32).astype(BF16)
    back = chosen(HALF * TILE, HALF * TILE, lambda r: (r % HALF) * TILE + r // HALF)
    for chunk in range(2):
        for block in range(2):
            starts = [
                (q // 4 * 2 + chunk) * run + q % 4 * length + block * TILE for q in range(HALF)
            ]
            rows = jnp.concatenate([change[start : start + TILE, :] for start in starts], axis=0)
            rows = jnp.dot(back, rows, preferred_element_type=F32).astype(BF16)
            for n in range(8):
                p, i = 2 * block + n // 4, n % 4
                tile = rows[n * TILE : (n + 1) * TILE]
                at = slice(chunk * TILE, (chunk + 1) * TILE)
                if outer_first:
                    outs[p][i, at] = tile
                else:
                    outs[i][p, at] = tile


def temporal(me, half, early, parts, wqkv, wo, outer_first):
    d = wo.shape[0]
    rows = HALF * 2 * TILE
    block = jax.ShapeDtypeStruct((4, 2 * TILE, d), BF16)
    return pl.pallas_call(
        functools.partial(temporal_kernel, half, outer_first),
        in_specs=[SMEM] + [VMEM] * 7,
        out_specs=[VMEM] * 4,
        out_shape=[block] * 4,
        scratch_shapes=[
            pltpu.VMEM((TILE * TILE, d), BF16),
            pltpu.VMEM((rows, d), BF16),
            pltpu.VMEM((2 * rows, 3 * d), BF16),
            pltpu.VMEM((2 * rows, d), BF16),
            pltpu.VMEM((2 * rows, d), BF16),
            pltpu.VMEM((16 * TILE, 16 * TILE), F32),
        ],
        compiler_params=pltpu.CompilerParams(vmem_limit_bytes=24 << 20),
        cost_estimate=pl.CostEstimate(
            flops=10 * rows * d * d + 32 * rows * GROUP * d,
            bytes_accessed=8 * d * d,
            transcendentals=2 * rows * GROUP * HEADS,
        ),
        name="temporal",
    )(me, early, *parts, wqkv, wo)


def last_kernel(me, mid01, mid23, *refs):
    early, late, out = refs[:4], refs[4:8], refs[8]
    number = me[0]
    f = pl.program_id(0)

    def add(mid, frame, at):
        for p in range(4):
            for i in range(4):
                owner = number ^ (OUTER[p] ^ INNER[i])
                rows = pl.ds(pl.multiple_of(owner * TILE, TILE), TILE)
                change = jnp.concatenate(
                    [
                        early[i][p].astype(F32)[at * HALF : (at + 1) * HALF],
                        late[p][i].astype(F32)[at * HALF : (at + 1) * HALF],
                    ],
                    axis=0,
                )
                out[0, rows, :] = (mid[frame, rows, :].astype(F32) + change).astype(BF16)

    for at in range(4):
        pl.when(f == at)(functools.partial(add, mid01 if at < 2 else mid23, at % 2, at))


def last(me, mid01, mid23, early, late):
    _, patches, d = mid01.shape
    return pl.pallas_call(
        last_kernel,
        grid=(4,),
        in_specs=[SMEM] + [VMEM] * 10,
        out_specs=pl.BlockSpec((1, patches, d), lambda f: (f, 0, 0)),
        out_shape=jax.ShapeDtypeStruct((4, patches, d), BF16),
        compiler_params=pltpu.CompilerParams(vmem_limit_bytes=16 << 20),
        cost_estimate=pl.CostEstimate(
            flops=patches * d * 4, bytes_accessed=patches * d * 8, transcendentals=0
        ),
        name="last",
    )(me, mid01, mid23, *early, *late)


def after(block, earlier):
    return lax.optimization_barrier((block, earlier))[0]


def exchange(pieces, masks):
    size = lax.axis_size("wide")
    return [pieces[0]] + [
        lax.ppermute(piece, "wide", [(w, w ^ mask) for w in range(size)])
        for piece, mask in zip(pieces[1:], masks[1:])
    ]


def shards(frames_in, qkv_spatial, out_spatial, qkv_temporal, out_temporal):
    me = lax.axis_index("wide").astype(jnp.int32).reshape(1)
    mid01, *pieces = spatial(me, frames_in, 0, 2, qkv_spatial, out_spatial, True, True)
    z_parts = exchange(regroup(exchange(pieces, OUTER)), INNER)
    mid23, *pieces = spatial(me, frames_in, 2, 2, qkv_spatial, out_spatial, False, False)
    first_half, second_half = halves(exchange(pieces, INNER))
    first_half = exchange(first_half, OUTER)
    projected = project_early(z_parts, qkv_temporal)
    pieces = temporal(me, 0, projected, first_half, qkv_temporal, out_temporal, True)
    early = exchange(regroup(exchange(pieces, OUTER)), INNER)
    second_half = after(second_half, projected)
    second_half = exchange(second_half, OUTER)
    pieces = temporal(me, 1, projected, second_half, qkv_temporal, out_temporal, False)
    late = exchange(regroup(exchange(pieces, INNER)), OUTER)
    return last(me, mid01, mid23, early, late)


def solution(mesh):
    wide = mesh.shape["wide"]

    def whole(frames_in, *weights):
        local = frames_in.shape[0] // (wide * mesh.shape["groups"])
        fits = wide == 16 and local == 4 and frames_in.shape[1] == wide * TILE
        return jax.shard_map(
            shards if fits else plain_shards,
            mesh=mesh,
            in_specs=(P(("groups", "wide"), None, None), P(), P(), P(), P()),
            out_specs=P(("groups", "wide"), None, None),
            check_vma=False,
        )(frames_in, *weights)

    return whole
```

```python
import functools

import jax
import jax.numpy as jnp
from jax import lax
from jax.experimental import pallas as pl
from jax.experimental.pallas import tpu as pltpu
from jax.sharding import PartitionSpec as P

HEADS = 12
HEAD_DIM = 64
LANES = 128
TILE = 16
HALF = TILE // 2
GROUP = 256
LAG = 1
BF16 = jnp.bfloat16
F32 = jnp.float32
VMEM = pl.BlockSpec(memory_space=pltpu.VMEM)
SMEM = pl.BlockSpec(memory_space=pltpu.SMEM)
HBM = pl.BlockSpec(memory_space=pltpu.HBM)

OUTER = (0, 12, 8, 4)
INNER = (0, 2, 3, 1)


def normalize(floats):
    average = jnp.mean(floats, axis=-1, keepdims=True)
    centred = floats - average
    spread = jnp.mean(centred * centred, axis=-1, keepdims=True)
    return (centred * lax.rsqrt(spread + 1e-06)).astype(BF16)


def project(flat_rows, matrix):
    return jnp.dot(flat_rows, matrix, preferred_element_type=F32)


def plain_attend(projected, score_form, mix_form):
    leading = projected.shape[:-1]
    split = projected.reshape(leading + (3, HEADS, HEAD_DIM))
    queries = split[..., 0, :, :]
    key_part = split[..., 1, :, :]
    values = split[..., 2, :, :]
    scores = jnp.einsum(
        score_form, queries, key_part, preferred_element_type=F32
    ) * HEAD_DIM ** (-0.5)
    weights = jax.nn.softmax(scores, axis=-1).astype(BF16)
    mixed = jnp.einsum(mix_form, weights, values, preferred_element_type=F32)
    return mixed.reshape(leading + (HEADS * HEAD_DIM,)).astype(BF16)


def attend_time(received):
    frame_total, single, item_count, columns = received.shape
    sequences = received.reshape(frame_total, item_count, columns)
    result = plain_attend(sequences, "qbhd,kbhd->bhqk", "bhqk,kbhd->qbhd")
    return result.reshape(frame_total, single, item_count, HEADS * HEAD_DIM)


def plain_shards(frames_in, qkv_spatial, out_spatial, qkv_temporal, out_temporal):
    frame_count, patch_count, features = frames_in.shape
    wide_count = lax.axis_size("wide")
    per_group = patch_count // wide_count
    first = normalize(frames_in.astype(F32))
    proj_one = project(first.reshape(-1, features), qkv_spatial).astype(BF16)
    proj_one = proj_one.reshape(frame_count, patch_count, 3 * features)
    spatial = plain_attend(proj_one, "bqhd,bkhd->bhqk", "bhqk,bkhd->bqhd")
    update = project(spatial.reshape(-1, features), out_spatial).reshape(
        frame_count, patch_count, features
    )
    middle = (frames_in.astype(F32) + update).astype(BF16)
    second = normalize(middle.astype(F32))
    grouped = second.reshape(frame_count, wide_count, per_group, features)
    received = lax.all_to_all(grouped, "wide", split_axis=1, concat_axis=0, tiled=True)
    frame_total, single, item_count, columns = received.shape
    local_proj = project(received.reshape(-1, columns), qkv_temporal).astype(BF16)
    local_proj = local_proj.reshape(frame_total, single, item_count, 3 * columns)
    temporal = attend_time(local_proj)
    returned = lax.all_to_all(temporal, "wide", split_axis=0, concat_axis=1, tiled=True)
    change = project(returned.reshape(-1, features), out_temporal).reshape(
        frame_count, patch_count, features
    )
    return (middle.astype(F32) + change).astype(BF16)


def project_rows(a, wqkv, qkv, places, j):
    d = a.shape[1]
    for start in range(j * d, (j + 1) * d, GROUP):
        cols = slice(start, start + GROUP)
        part = jnp.dot(a[...], wqkv[:, cols], preferred_element_type=F32).astype(BF16)
        part = part * BF16(HEAD_DIM**-0.5) if j == 0 else part
        size = a.shape[0] // len(places)
        for n, place in enumerate(places):
            qkv[place : place + size, cols] = part[n * size : (n + 1) * size]


def attend(qkv, mixed, blocks, bias=None):
    d = mixed.shape[1]
    units = [(r, c, half) for r in blocks for c in range(0, d, LANES) for half in range(2)]
    size = blocks[0].stop - blocks[0].start
    low = lax.broadcasted_iota(jnp.int32, (size, LANES), 1) < HEAD_DIM
    begun, sums = {}, {}

    def begin(n):
        r, c, half = units[n]
        q = qkv[r, c : c + LANES]
        one = jnp.where(low if half == 0 else ~low, q, jnp.zeros_like(q))
        scores = lax.dot_general(
            one,
            qkv[r, d + c : d + c + LANES],
            (((1,), (1,)), ((), ())),
            preferred_element_type=F32,
        )
        if bias is not None:
            scores = scores + bias[...]
        begun[n] = scores, jnp.max(scores, axis=-1, keepdims=True)

    def end(n):
        r, c, half = units[n]
        scores, top = begun.pop(n)
        weights = jnp.exp(scores - top).astype(BF16)
        v = qkv[r, 2 * d + c : 2 * d + c + LANES]
        values = jnp.where(low if half == 0 else ~low, v, jnp.ones_like(v))
        sums[half] = jnp.dot(weights, values, preferred_element_type=F32)
        if half == 1:
            total = pltpu.roll(jnp.where(low, sums[1], sums[0]), HEAD_DIM, 1)
            mixed[r, c : c + LANES] = (jnp.where(low, sums[0], sums[1]) / total).astype(BF16)

    for n in range(len(units) + LAG):
        if n < len(units):
            begin(n)
        if n >= LAG:
            end(n - LAG)


def spatial_kernel(outer_first, begin, fetch, me, x_in, wqkv_in, wo_in, middle, *refs):
    frames, patches, d = middle.shape
    outs, (a, qkv, mixed, second, *held) = refs[:4], refs[4:]
    number = me[0]
    if fetch:
        x, wqkv, wo, sems = held
        pairs = [(x_in.at[begin + f], x.at[f]) for f in range(frames)]
        pairs += [(wqkv_in.at[:, pl.ds(j * d, d)], wqkv.at[:, pl.ds(j * d, d)]) for j in range(3)]
        pairs += [(wo_in, wo)]
        copies = [pltpu.make_async_copy(*pair, sems.at[n]) for n, pair in enumerate(pairs)]
        for copy in copies:
            copy.start()
    else:
        x, wqkv, wo = x_in.at[pl.ds(begin, frames)], wqkv_in, wo_in
    for f in range(frames):
        if fetch:
            copies[f].wait()
        a[f * patches : (f + 1) * patches, :] = normalize(x[f].astype(F32))
    for j in range(3):
        if fetch:
            copies[frames + j].wait()
        project_rows(a, wqkv, qkv, (0,), j)
    if fetch:
        copies[frames + 3].wait()
    attend(qkv, mixed, [slice(f * patches, (f + 1) * patches) for f in range(frames)])
    for f in range(frames):
        r = slice(f * patches, (f + 1) * patches)
        update = jnp.dot(mixed[r, :], wo[...], preferred_element_type=F32)
        mid = (x[f].astype(F32) + update).astype(BF16)
        middle[f] = mid
        second[...] = normalize(mid.astype(F32))
        for p in range(4):
            for i in range(4):
                owner = number ^ (OUTER[p] ^ INNER[i])
                rows = second[pl.ds(pl.multiple_of(owner * TILE, TILE), TILE), :]
                if outer_first:
                    outs[p][f, i] = rows
                else:
                    outs[i][f, p] = rows


def spatial(me, x, begin, frames, wqkv, wo, outer_first, fetch):
    _, patches, d = x.shape
    rows = frames * patches
    block = jax.ShapeDtypeStruct((frames, 4, TILE, d), BF16)
    held = [
        pltpu.VMEM((frames, patches, d), BF16),
        pltpu.VMEM(wqkv.shape, BF16),
        pltpu.VMEM(wo.shape, BF16),
        pltpu.SemaphoreType.DMA((frames + 4,)),
    ]
    return pl.pallas_call(
        functools.partial(spatial_kernel, outer_first, begin, fetch),
        in_specs=[SMEM] + [HBM if fetch else VMEM] * 3,
        out_specs=[VMEM] * 5,
        out_shape=[jax.ShapeDtypeStruct((frames, patches, d), BF16)] + [block] * 4,
        scratch_shapes=[
            pltpu.VMEM((rows, d), BF16),
            pltpu.VMEM((rows, 3 * d), BF16),
            pltpu.VMEM((rows, d), BF16),
            pltpu.VMEM((patches, d), BF16),
        ]
        + (held if fetch else []),
        compiler_params=pltpu.CompilerParams(vmem_limit_bytes=(52 if fetch else 24) << 20),
        cost_estimate=pl.CostEstimate(
            flops=8 * rows * d * d + 16 * rows * patches * d,
            bytes_accessed=8 * d * d,
            transcendentals=rows * patches * HEADS,
        ),
        name="spatial_outer" if outer_first else "spatial_inner",
    )(me, x, wqkv, wo)


def regroup_kernel(*refs):
    ins, outs = refs[:4], refs[4:]
    for b in range(4):
        for a in range(4):
            if len(ins[0].shape) == 4:
                outs[b][a] = ins[a][:, b]
            else:
                outs[b][a] = ins[a][b]


def regroup(pieces):
    shape = pieces[0].shape
    shape = (4, shape[0]) + shape[2:] if len(shape) == 4 else shape
    return pl.pallas_call(
        regroup_kernel,
        in_specs=[VMEM] * 4,
        out_specs=[VMEM] * 4,
        out_shape=[jax.ShapeDtypeStruct(shape, BF16)] * 4,
        compiler_params=pltpu.CompilerParams(vmem_limit_bytes=4 << 20),
        cost_estimate=pl.CostEstimate(flops=0, bytes_accessed=1 << 20, transcendentals=0),
        name="regroup",
    )(*pieces)


def halves_kernel(*refs):
    ins, outs = refs[:4], refs[4:]
    for i in range(4):
        for p in range(4):
            tiles = [ins[i][f, p].astype(F32) for f in range(2)]
            for half in range(2):
                rows = [tile[half * HALF : (half + 1) * HALF] for tile in tiles]
                outs[4 * half + p][i] = jnp.concatenate(rows, axis=0).astype(BF16)


def halves(pieces):
    shape = (4,) + pieces[0].shape[2:]
    blocks = pl.pallas_call(
        halves_kernel,
        in_specs=[VMEM] * 4,
        out_specs=[VMEM] * 8,
        out_shape=[jax.ShapeDtypeStruct(shape, BF16)] * 8,
        compiler_params=pltpu.CompilerParams(vmem_limit_bytes=4 << 20),
        cost_estimate=pl.CostEstimate(flops=0, bytes_accessed=1 << 20, transcendentals=0),
        name="halves",
    )(*pieces)
    return blocks[:4], blocks[4:]


def chosen(rows, columns, source):
    r = lax.broadcasted_iota(jnp.int32, (rows, columns), 0)
    c = lax.broadcasted_iota(jnp.int32, (rows, columns), 1)
    return (c == source(r)).astype(F32).astype(BF16)


def project_kernel(*refs):
    parts, wqkv, qkv, scratch, a = refs[:4], *refs[4:]
    length = 2 * TILE
    pick = chosen(TILE * TILE, TILE * TILE, lambda r: r % TILE * TILE + r // TILE)
    for block in range(2):
        for n in range(TILE):
            p, i, f = 2 * block + n // 8, n // 2 % 4, n % 2
            scratch[n * TILE : (n + 1) * TILE, :] = parts[i][p, f]
        taken = jnp.dot(pick, scratch[...], preferred_element_type=F32).astype(BF16)
        for q in range(TILE):
            start = q * length + block * TILE
            a[start : start + TILE, :] = taken[q * TILE : (q + 1) * TILE]
    for j in range(3):
        project_rows(a, wqkv, qkv, (0,), j)


def project_early(parts, wqkv):
    d = wqkv.shape[0]
    rows = TILE * 2 * TILE
    return pl.pallas_call(
        project_kernel,
        in_specs=[VMEM] * 5,
        out_specs=VMEM,
        out_shape=jax.ShapeDtypeStruct((rows, 3 * d), BF16),
        scratch_shapes=[pltpu.VMEM((TILE * TILE, d), BF16), pltpu.VMEM((rows, d), BF16)],
        compiler_params=pltpu.CompilerParams(vmem_limit_bytes=24 << 20),
        cost_estimate=pl.CostEstimate(
            flops=6 * rows * d * d, bytes_accessed=6 * d * d, transcendentals=0
        ),
        name="project_early",
    )(*parts, wqkv)


def temporal_kernel(half, outer_first, me, early, *refs):
    parts, wqkv, wo, outs = refs[:4], refs[4], refs[5], refs[6:10]
    scratch, a, qkv, mixed, change, bias = refs[10:]
    length = 2 * TILE
    run = 4 * length
    row, column = (lax.broadcasted_iota(jnp.int32, bias.shape, axis) for axis in range(2))
    other = ((row ^ column) & (run - length)) != 0
    bias[...] = jnp.where(other, -jnp.inf, 0.0)
    for p in range(4):
        for i in range(4):
            start = (4 * p + i) * TILE
            scratch[start : start + TILE, :] = parts[p][i]
    pick = chosen(
        HALF * length,
        HALF * length,
        lambda r: r % length // 2 * TILE + r % 2 * HALF + r // length,
    )
    a[...] = jnp.dot(pick, scratch[...], preferred_element_type=F32).astype(BF16)
    groups = range(HALF // 4)
    for g in groups:
        first = (half * HALF + 4 * g) * length
        qkv[2 * g * run : (2 * g + 1) * run, :] = early[first : first + run, :]
    for j in range(3):
        project_rows(a, wqkv, qkv, [(2 * g + 1) * run for g in groups], j)
    attend(qkv, mixed, [slice(2 * g * run, 2 * (g + 1) * run) for g in groups], bias)
    change[...] = jnp.dot(mixed[...], wo[...], preferred_element_type=F32).astype(BF16)
    back = chosen(HALF * TILE, HALF * TILE, lambda r: (r % HALF) * TILE + r // HALF)
    for chunk in range(2):
        for block in range(2):
            starts = [
                (q // 4 * 2 + chunk) * run + q % 4 * length + block * TILE for q in range(HALF)
            ]
            rows = jnp.concatenate([change[start : start + TILE, :] for start in starts], axis=0)
            rows = jnp.dot(back, rows, preferred_element_type=F32).astype(BF16)
            for n in range(8):
                p, i = 2 * block + n // 4, n % 4
                tile = rows[n * TILE : (n + 1) * TILE]
                at = slice(chunk * TILE, (chunk + 1) * TILE)
                if outer_first:
                    outs[p][i, at] = tile
                else:
                    outs[i][p, at] = tile


def temporal(me, half, early, parts, wqkv, wo, outer_first):
    d = wo.shape[0]
    rows = HALF * 2 * TILE
    block = jax.ShapeDtypeStruct((4, 2 * TILE, d), BF16)
    return pl.pallas_call(
        functools.partial(temporal_kernel, half, outer_first),
        in_specs=[SMEM] + [VMEM] * 7,
        out_specs=[VMEM] * 4,
        out_shape=[block] * 4,
        scratch_shapes=[
            pltpu.VMEM((TILE * TILE, d), BF16),
            pltpu.VMEM((rows, d), BF16),
            pltpu.VMEM((2 * rows, 3 * d), BF16),
            pltpu.VMEM((2 * rows, d), BF16),
            pltpu.VMEM((2 * rows, d), BF16),
            pltpu.VMEM((16 * TILE, 16 * TILE), F32),
        ],
        compiler_params=pltpu.CompilerParams(vmem_limit_bytes=24 << 20),
        cost_estimate=pl.CostEstimate(
            flops=10 * rows * d * d + 32 * rows * GROUP * d,
            bytes_accessed=8 * d * d,
            transcendentals=2 * rows * GROUP * HEADS,
        ),
        name="temporal",
    )(me, early, *parts, wqkv, wo)


def last_kernel(me, mid01, mid23, *refs):
    early, late, out = refs[:4], refs[4:8], refs[8]
    number = me[0]
    f = pl.program_id(0)

    def add(mid, frame, at):
        for p in range(4):
            for i in range(4):
                owner = number ^ (OUTER[p] ^ INNER[i])
                rows = pl.ds(pl.multiple_of(owner * TILE, TILE), TILE)
                change = jnp.concatenate(
                    [
                        early[i][p].astype(F32)[at * HALF : (at + 1) * HALF],
                        late[p][i].astype(F32)[at * HALF : (at + 1) * HALF],
                    ],
                    axis=0,
                )
                out[0, rows, :] = (mid[frame, rows, :].astype(F32) + change).astype(BF16)

    for at in range(4):
        pl.when(f == at)(functools.partial(add, mid01 if at < 2 else mid23, at % 2, at))


def last(me, mid01, mid23, early, late):
    _, patches, d = mid01.shape
    return pl.pallas_call(
        last_kernel,
        grid=(4,),
        in_specs=[SMEM] + [VMEM] * 10,
        out_specs=pl.BlockSpec((1, patches, d), lambda f: (f, 0, 0)),
        out_shape=jax.ShapeDtypeStruct((4, patches, d), BF16),
        compiler_params=pltpu.CompilerParams(vmem_limit_bytes=16 << 20),
        cost_estimate=pl.CostEstimate(
            flops=patches * d * 4, bytes_accessed=patches * d * 8, transcendentals=0
        ),
        name="last",
    )(me, mid01, mid23, *early, *late)


def after(block, earlier):
    return lax.optimization_barrier((block, earlier))[0]


def exchange(pieces, masks):
    size = lax.axis_size("wide")
    return [pieces[0]] + [
        lax.ppermute(piece, "wide", [(w, w ^ mask) for w in range(size)])
        for piece, mask in zip(pieces[1:], masks[1:])
    ]


def shards(frames_in, qkv_spatial, out_spatial, qkv_temporal, out_temporal):
    me = lax.axis_index("wide").astype(jnp.int32).reshape(1)
    mid01, *pieces = spatial(me, frames_in, 0, 2, qkv_spatial, out_spatial, True, True)
    z_parts = exchange(regroup(exchange(pieces, OUTER)), INNER)
    mid23, *pieces = spatial(me, frames_in, 2, 2, qkv_spatial, out_spatial, False, False)
    first_half, second_half = halves(exchange(pieces, INNER))
    first_half = exchange(first_half, OUTER)
    projected = project_early(z_parts, qkv_temporal)
    pieces = temporal(me, 0, projected, first_half, qkv_temporal, out_temporal, True)
    early = exchange(regroup(exchange(pieces, OUTER)), INNER)
    second_half = after(second_half, projected)
    second_half = exchange(second_half, OUTER)
    pieces = temporal(me, 1, projected, second_half, qkv_temporal, out_temporal, False)
    late = exchange(regroup(exchange(pieces, INNER)), OUTER)
    return last(me, mid01, mid23, early, late)


def solution(mesh):
    wide = mesh.shape["wide"]

    def whole(frames_in, *weights):
        local = frames_in.shape[0] // (wide * mesh.shape["groups"])
        fits = wide == 16 and local == 4 and frames_in.shape[1] == wide * TILE
        return jax.shard_map(
            shards if fits else plain_shards,
            mesh=mesh,
            in_specs=(P(("groups", "wide"), None, None), P(), P(), P(), P()),
            out_specs=P(("groups", "wide"), None, None),
            check_vma=False,
        )(frames_in, *weights)

    return whole
```
